512 devices in a mesh: row: 16 (over z), col: 8 (over x, core), layer: 4 (over y).
Axes of the slice: x: 4, y: 4, z: 16, core: 2. Of those that a mesh axis runs over, the one named last changes fastest.
Arguments:
- a_blocks: bfloat16 [8192, 16384], P('col', ('layer', 'row')), may hold values from -6 to 6
- a_mask: int32 [128, 256], P('col', ('layer', 'row')), may hold values from 0 to 1, as said below
- b_blocks: bfloat16 [16384, 8192], P(('layer', 'col'), 'row'), may hold values from -0.0625 to 0.0625
- b_mask: int32 [256, 128], P(('layer', 'col'), 'row'), may hold values 0 or 1
- c_mask: int32 [128, 128], P('col', 'row'), may hold values 0 or 1
Outputs:
- product: float32 [8192, 8192], P(('col', 'layer'), 'row')
The draws below stay inside these ranges and needn't reach their ends.
Inputs may be any that keep to these rules, and one draw needn't show every extreme that they name: `a_mask`: 0 or 1; each row of blocks has its own share of occupied blocks.
All inputs are finite; a program needn't handle non-finite values. No bound on the sum of `b_mask` or of `c_mask` on one device may be relied on, other than what follows from the above.
Results may differ from the reference program's by a relative error of at most 0.0003.
Values may be sent and summed in bfloat16 or wider, within the bound.
A program may use at most 64 MiB of HBM per device.

```python
import jax
import jax.numpy as jnp

BLK = 64
MT = 128
NT = 128
KTOT = 256


def draw_a_mask(key, part):
    key = jax.random.fold_in(key, 7)
    first, second = jax.random.split(key)
    levels = jax.random.randint(first, (MT, 1), 1, 10)
    cells = jax.random.randint(second, (MT, KTOT), 0, 10)
    return (cells < levels).astype(jnp.int32)


def plant(array, own_key, least, high):
    longest = array.shape.index(max(array.shape))
    spots = []
    for shift in (0, 1):
        where = [jax.random.randint(jax.random.fold_in(own_key, axis), (), 0, length) for axis, length in enumerate(array.shape)]
        where[longest] = (where[longest] + shift) % array.shape[longest]
        spots.append(tuple(where))
    return array.at[spots[0]].set(least).at[spots[1]].set(high)


def shard_levels(rng, dims, pieces, least, high):
    def one(position, shards_of):
        draws = jax.random.uniform(jax.random.fold_in(jax.random.fold_in(rng, 6), position), (shards_of,), jnp.float32, least / len(pieces), high / len(pieces))
        return jnp.repeat(jnp.exp(draws), dims[position] // shards_of).reshape((-1,) + (1,) * (len(dims) - position - 1))

    level = one(*pieces[0])
    for cut in pieces[1:]:
        level = level * one(*cut)
    return level


def scatter_about(key, shape, scale, bound, cuts=(), kind=jnp.bfloat16):
    level = shard_levels(key, shape, cuts, -0.22, 0.18) if cuts else 1.0
    result = jax.random.normal(key, shape, jnp.float32) * scale * level
    return jnp.minimum(jnp.maximum(result, -bound), bound).astype(kind)


def setup_inputs(seed: int = 0) -> dict:
    splits = jax.random.split(jax.random.key(seed), 6)
    a_blocks = scatter_about(splits[0], (MT * BLK, KTOT * BLK), 1.0, 6.0, ((0, 8), (1, 64)))
    a_mask = draw_a_mask(jax.random.fold_in(splits[5], 71), 0)
    b_blocks = scatter_about(splits[2], (KTOT * BLK, NT * BLK), (KTOT * BLK // 2) ** -0.5, 0.0625, ((0, 32), (1, 16)))
    b_mask = plant((jax.random.randint(splits[3], (KTOT, NT), 0, 2) < 1).astype(jnp.int32), jax.random.fold_in(splits[3], 1), 0, 1)
    c_mask = plant((jax.random.randint(splits[4], (MT, NT), 0, 4) < 3).astype(jnp.int32), jax.random.fold_in(splits[4], 1), 0, 1)
    return {"a_blocks": a_blocks, "a_mask": a_mask, "b_blocks": b_blocks, "b_mask": b_mask, "c_mask": c_mask}


def expand_mask(mask, dtype):
    return jnp.repeat(jnp.repeat(mask, BLK, axis=0), BLK, axis=1).astype(dtype)


def reference(a_blocks, a_mask, b_blocks, b_mask, c_mask):
    masked_a = a_blocks * expand_mask(a_mask, jnp.bfloat16)
    masked_b = b_blocks * expand_mask(b_mask, jnp.bfloat16)
    full = jnp.dot(masked_a, masked_b, preferred_element_type=jnp.float32)
    return full * expand_mask(c_mask, jnp.float32)
```

```python
import functools

import jax
import jax.numpy as jnp
from jax import lax
from jax.experimental import pallas as pl
from jax.experimental.pallas import tpu as pltpu
from jax.sharding import PartitionSpec as P

BLK = 64
MESH = pl.DeviceIdType.MESH
ORDER = (1, 3, 2, 0)


def wrap(value, size):
    return lax.rem(value + size, size)


def kernel(
    nz, nx, ny,
    a_mask, b_mask, c_mask, a_ref, b_ref, out_ref,
    am, g, bf, acc, got,
    a_send, a_recv, b_send, b_recv, c_send, c_recv,
):
    z, col, y = lax.axis_index("row"), lax.axis_index("col"), lax.axis_index("layer")
    x, core = col // 2, lax.rem(col, 2)
    half = nz // 2
    rows, depth = a_ref.shape
    grp = rows // ny
    sub = grp // 2
    bdepth, ncols = b_ref.shape

    zs = (wrap(z + 1, nz), wrap(z - 1, nz))
    xs = (wrap(x + 1, nx) * 2 + core, wrap(x - 1, nx) * 2 + core)
    sib = x * 2 + 1 - core
    opp = wrap(x + 2, nx) * 2 + core

    barrier = pltpu.get_barrier_semaphore()
    for peer in zs:
        pl.semaphore_signal(barrier, inc=1, device_id={"row": peer}, device_id_type=MESH)
    for peer in xs + (sib,):
        pl.semaphore_signal(barrier, inc=1, device_id={"col": peer}, device_id_type=MESH)
    for d in range(1, ny):
        pl.semaphore_signal(barrier, inc=1, device_id={"layer": wrap(y + d, ny)}, device_id_type=MESH)

    lane = lax.broadcasted_iota(jnp.int32, (1, 2 * BLK), 1)

    def pair(m0, m1):
        return jnp.where(lane < BLK, m0, m1).astype(jnp.float32)

    def group_of(q):
        d = jnp.where(q == 0, ORDER[0], jnp.where(q == 1, ORDER[1], jnp.where(q == 2, ORDER[2], 0)))
        return wrap(y + d, ny), d

    nb = grp // BLK
    def mask_a(t, _):
        q, r = t // nb, lax.rem(t, nb)
        src = group_of(q)[0] * nb + r
        at = pl.ds(pl.multiple_of(src * BLK, BLK), BLK)
        to = pl.ds(pl.multiple_of(t * BLK, BLK), BLK)
        for p in range(depth // (2 * BLK)):
            ls = slice(p * 2 * BLK, (p + 1) * 2 * BLK)
            m = pair(a_mask[src, 2 * p], a_mask[src, 2 * p + 1]).astype(am.dtype)
            am[to, ls] = a_ref[at, ls] * m
        return 0
    lax.fori_loop(0, rows // BLK, mask_a, 0)

    def mask_b(t, _):
        at = pl.ds(pl.multiple_of(t * BLK, BLK), BLK)
        to = pl.ds(pl.multiple_of(col * bdepth + t * BLK, BLK), BLK)
        for p in range(ncols // (2 * BLK)):
            ls = slice(p * 2 * BLK, (p + 1) * 2 * BLK)
            m = pair(b_mask[t, 2 * p], b_mask[t, 2 * p + 1]).astype(bf.dtype)
            bf[to, ls] = b_ref[at, ls] * m
        return 0
    lax.fori_loop(0, bdepth // BLK, mask_b, 0)

    pl.semaphore_wait(barrier, 5 + ny - 1)

    def chunk(ref, q, s):
        return ref.at[pl.ds(pl.multiple_of(q * grp + s * sub, sub), sub)]

    def hop(way, q, s, h):
        dst = chunk(g.at[way, h - 1], q, s)
        return dst, pltpu.make_async_remote_copy(
            src_ref=dst, dst_ref=dst,
            send_sem=a_send.at[way, q, s, h - 1], recv_sem=a_recv.at[way, q, s, h - 1],
            device_id={"row": zs[way]}, device_id_type=MESH,
        )

    def start_hop(way, q, s, h):
        dst = chunk(g.at[way, h - 1], q, s)
        def go(src):
            pltpu.make_async_remote_copy(
                src_ref=src, dst_ref=dst,
                send_sem=a_send.at[way, q, s, h - 1], recv_sem=a_recv.at[way, q, s, h - 1],
                device_id={"row": zs[way]}, device_id_type=MESH,
            ).start()
        @pl.when(h == 1)
        def _():
            go(chunk(am, q, s))
        @pl.when(h > 1)
        def _():
            go(chunk(g.at[way, jnp.maximum(h - 2, 0)], q, s))

    def b_rows(owner, first, count):
        return bf.at[pl.ds(pl.multiple_of(owner * bdepth + first, count), count)]

    hb = bdepth // 2
    def b_copy(n, owner, first, count, peer):
        ref = b_rows(owner, first, count)
        return pltpu.make_async_remote_copy(
            src_ref=ref, dst_ref=ref, send_sem=b_send.at[n], recv_sem=b_recv.at[n],
            device_id={"col": peer}, device_id_type=MESH,
        )

    b_out = (
        b_copy(0, col, 0, bdepth, xs[0]),
        b_copy(1, col, 0, bdepth, xs[1]),
        b_copy(2, xs[1], 0, hb, xs[0]),
        b_copy(3, xs[0], hb, hb, xs[1]),
        b_copy(4, col, 0, bdepth, sib),
        b_copy(5, xs[1], 0, bdepth, sib),
        b_copy(6, xs[0], 0, bdepth, sib),
        b_copy(7, opp, 0, bdepth, sib),
    )
    other = 1 - 2 * core
    b_in = (
        b_copy(0, xs[1], 0, bdepth, xs[0]),
        b_copy(1, xs[0], 0, bdepth, xs[1]),
        b_copy(2, opp, 0, hb, xs[0]),
        b_copy(3, opp, hb, hb, xs[1]),
        b_copy(4, sib, 0, bdepth, sib),
        b_copy(5, xs[1] + other, 0, bdepth, sib),
        b_copy(6, xs[0] + other, 0, bdepth, sib),
        b_copy(7, opp + other, 0, bdepth, sib),
    )

    def c_copy(q):
        target, d = group_of(q)
        return pltpu.make_async_remote_copy(
            src_ref=acc.at[q], dst_ref=got.at[q], send_sem=c_send.at[q], recv_sem=c_recv.at[q],
            device_id={"layer": target}, device_id_type=MESH,
        )

    def b_of(source):
        return bf[pl.ds(pl.multiple_of(source * depth, depth), depth), :]

    def dot(a, b):
        return jnp.dot(a, b, preferred_element_type=jnp.float32)

    def work(q, h):
        @pl.when(h == 0)
        def _():
            acc[q] = dot(am[pl.ds(pl.multiple_of(q * grp, grp), grp), :], b_of(z))
        @pl.when((h > 0) & (h < half))
        def _():
            at = pl.ds(pl.multiple_of(q * grp, grp), grp)
            n = jnp.maximum(h - 1, 0)
            acc[q] += dot(g[0, n, at, :], b_of(wrap(z - h, nz))) + dot(g[1, n, at, :], b_of(wrap(z + h, nz)))
        @pl.when(h == half)
        def _():
            source = b_of(wrap(z + half, nz))
            for s in range(2):
                at = pl.ds(pl.multiple_of(q * grp + s * sub, sub), sub)
                to = pl.ds(s * sub, sub)
                acc[q, to, :] += dot(g[s, half - 1, at, :], source)

    def settle(q):
        for s in range(2):
            hop(s, q, s, half)[1].wait_recv()

    def step(t, _):
        q, h = t // half, lax.rem(t, half) + 1
        for s in range(2):
            for way in range(2):
                @pl.when(h > 1)
                def _():
                    hop(way, q, s, jnp.maximum(h - 1, 1))[1].wait_recv()
                if way == s:
                    start_hop(way, q, s, h)
                else:
                    @pl.when(h < half)
                    def _():
                        start_hop(way, q, s, h)

        @pl.when(t == 0)
        def _():
            for n in (0, 1, 4):
                b_out[n].start()

        @pl.when((q == 0) & (h == 6))
        def _():
            for n in (0, 1):
                b_in[n].wait_recv()
            for n in (2, 3, 5, 6):
                b_out[n].start()

        @pl.when((q >= 1) & (h == 1))
        def _():
            settle(q - 1)

        @pl.when((q == 1) & (h == 1))
        def _():
            for n in (2, 3):
                b_in[n].wait_recv()
            b_out[7].start()
            for n in range(4, 8):
                b_in[n].wait_recv()

        @pl.when(q >= 1)
        def _():
            @pl.when((h == 1) & (q >= 2))
            def _():
                work(q - 1, half)
                c_copy(q - 1).start()
            work(q, h - 1)

        @pl.when(q == 1)
        def _():
            work(0, h - 1)
            @pl.when(h == half)
            def _():
                work(0, half)
                c_copy(0).start()
        return 0

    lax.fori_loop(0, ny * half, step, 0)
    last = ny - 1
    settle(last)
    work(last, half)
    for q in range(last):
        c_copy(q).wait_recv()
    for r in range(nb):
        at = pl.ds(r * BLK, BLK)
        for p in range(ncols // (2 * BLK)):
            ls = slice(p * 2 * BLK, (p + 1) * 2 * BLK)
            row = y * nb + r
            total = acc[last, at, ls] + got[0, at, ls] + got[1, at, ls] + got[2, at, ls]
            out_ref[at, ls] = total * pair(c_mask[row, 2 * p], c_mask[row, 2 * p + 1])

    def sent(t, _):
        q, h = t // half, lax.rem(t, half) + 1
        for s in range(2):
            for way in range(2):
                if way == s:
                    hop(way, q, s, h)[1].wait_send()
                else:
                    @pl.when(h < half)
                    def _():
                        hop(way, q, s, h)[1].wait_send()
        return 0
    lax.fori_loop(0, ny * half, sent, 0)
    for copy in b_out:
        copy.wait_send()
    for q in range(last):
        c_copy(q).wait_send()


def shards(nz, nx, ny, a_blocks, a_mask, b_blocks, b_mask, c_mask):
    rows, depth = a_blocks.shape
    bdepth, ncols = b_blocks.shape
    grp = rows // ny
    half = nz // 2
    vmem, smem = pl.BlockSpec(memory_space=pltpu.VMEM), pl.BlockSpec(memory_space=pltpu.SMEM)
    dma = pltpu.SemaphoreType.DMA
    return pl.pallas_call(
        functools.partial(kernel, nz, nx, ny),
        out_shape=jax.ShapeDtypeStruct((grp, ncols), jnp.float32),
        in_specs=[smem, smem, smem, vmem, vmem],
        out_specs=vmem,
        scratch_shapes=[
            pltpu.VMEM((rows, depth), jnp.bfloat16),
            pltpu.VMEM((2, half, rows, depth), jnp.bfloat16),
            pltpu.VMEM((2 * nx * bdepth, ncols), jnp.bfloat16),
            pltpu.VMEM((ny, grp, ncols), jnp.float32),
            pltpu.VMEM((ny - 1, grp, ncols), jnp.float32),
            dma((2, ny, 2, half)),
            dma((2, ny, 2, half)),
            dma((8,)),
            dma((8,)),
            dma((ny - 1,)),
            dma((ny - 1,)),
        ],
        compiler_params=pltpu.CompilerParams(
            collective_id=0, has_side_effects=True, vmem_limit_bytes=40 * 2**20
        ),
    )(a_mask, b_mask, c_mask, a_blocks, b_blocks)


def solution(mesh):
    nz, ncol, ny = mesh.shape["row"], mesh.shape["col"], mesh.shape["layer"]
    in_specs = (
        P("col", ("layer", "row")),
        P("col", ("layer", "row")),
        P(("layer", "col"), "row"),
        P(("layer", "col"), "row"),
        P("col", "row"),
    )
    out_specs = P(("col", "layer"), "row")
    body = functools.partial(shards, nz, ncol // 2, ny)
    return jax.shard_map(body, mesh=mesh, in_specs=in_specs, out_specs=out_specs, check_vma=False)
```

```python
import functools

import jax
import jax.numpy as jnp
from jax import lax
from jax.experimental import pallas as pl
from jax.experimental.pallas import tpu as pltpu
from jax.sharding import PartitionSpec as P

BLK = 64
MESH = pl.DeviceIdType.MESH
ORDER = (1, 3, 2, 0)

TILES = ((4, 4), (4, 4), (3, 2), (2, 3))
NTILES = sum(map(sum, TILES))
UPTO = tuple(sum(map(sum, TILES[: q + 1])) for q in range(4))


def wrap(value, size):
    return lax.rem(value + size, size)


def dense_kernel(
    nz, nx, ny,
    a_mask, b_mask, c_mask, a_ref, b_ref, out_ref,
    am, g, bf, acc, got,
    a_send, a_recv, b_send, b_recv, c_send, c_recv,
):
    z, col, y = lax.axis_index("row"), lax.axis_index("col"), lax.axis_index("layer")
    x, core = col // 2, lax.rem(col, 2)
    half = nz // 2
    rows, depth = a_ref.shape
    grp = rows // ny
    sub = grp // 2
    bdepth, ncols = b_ref.shape

    zs = (wrap(z + 1, nz), wrap(z - 1, nz))
    xs = (wrap(x + 1, nx) * 2 + core, wrap(x - 1, nx) * 2 + core)
    sib = x * 2 + 1 - core
    opp = wrap(x + 2, nx) * 2 + core

    barrier = pltpu.get_barrier_semaphore()
    for peer in zs:
        pl.semaphore_signal(barrier, inc=1, device_id={"row": peer}, device_id_type=MESH)
    for peer in xs + (sib,):
        pl.semaphore_signal(barrier, inc=1, device_id={"col": peer}, device_id_type=MESH)
    for d in range(1, ny):
        pl.semaphore_signal(barrier, inc=1, device_id={"layer": wrap(y + d, ny)}, device_id_type=MESH)

    lane = lax.broadcasted_iota(jnp.int32, (1, 2 * BLK), 1)

    def pair(m0, m1):
        return jnp.where(lane < BLK, m0, m1).astype(jnp.float32)

    def group_of(q):
        d = jnp.where(q == 0, ORDER[0], jnp.where(q == 1, ORDER[1], jnp.where(q == 2, ORDER[2], 0)))
        return wrap(y + d, ny), d

    nb = grp // BLK
    def mask_a(t, _):
        q, r = t // nb, lax.rem(t, nb)
        src = group_of(q)[0] * nb + r
        at = pl.ds(pl.multiple_of(src * BLK, BLK), BLK)
        to = pl.ds(pl.multiple_of(t * BLK, BLK), BLK)
        for p in range(depth // (2 * BLK)):
            ls = slice(p * 2 * BLK, (p + 1) * 2 * BLK)
            m = pair(a_mask[src, 2 * p], a_mask[src, 2 * p + 1]).astype(am.dtype)
            am[to, ls] = a_ref[at, ls] * m
        return 0
    lax.fori_loop(0, rows // BLK, mask_a, 0)

    def mask_b(t, _):
        at = pl.ds(pl.multiple_of(t * BLK, BLK), BLK)
        to = pl.ds(pl.multiple_of(col * bdepth + t * BLK, BLK), BLK)
        for p in range(ncols // (2 * BLK)):
            ls = slice(p * 2 * BLK, (p + 1) * 2 * BLK)
            m = pair(b_mask[t, 2 * p], b_mask[t, 2 * p + 1]).astype(bf.dtype)
            bf[to, ls] = b_ref[at, ls] * m
        return 0
    lax.fori_loop(0, bdepth // BLK, mask_b, 0)

    pl.semaphore_wait(barrier, 5 + ny - 1)

    def chunk(ref, q, s):
        return ref.at[pl.ds(pl.multiple_of(q * grp + s * sub, sub), sub)]

    def hop(way, q, s, h):
        dst = chunk(g.at[way, h - 1], q, s)
        return dst, pltpu.make_async_remote_copy(
            src_ref=dst, dst_ref=dst,
            send_sem=a_send.at[way, q, s, h - 1], recv_sem=a_recv.at[way, q, s, h - 1],
            device_id={"row": zs[way]}, device_id_type=MESH,
        )

    def start_hop(way, q, s, h):
        dst = chunk(g.at[way, h - 1], q, s)
        def go(src):
            pltpu.make_async_remote_copy(
                src_ref=src, dst_ref=dst,
                send_sem=a_send.at[way, q, s, h - 1], recv_sem=a_recv.at[way, q, s, h - 1],
                device_id={"row": zs[way]}, device_id_type=MESH,
            ).start()
        @pl.when(h == 1)
        def _():
            go(chunk(am, q, s))
        @pl.when(h > 1)
        def _():
            go(chunk(g.at[way, jnp.maximum(h - 2, 0)], q, s))

    def b_rows(owner, first, count):
        return bf.at[pl.ds(pl.multiple_of(owner * bdepth + first, count), count)]

    hb = bdepth // 2
    def b_copy(n, owner, first, count, peer):
        ref = b_rows(owner, first, count)
        return pltpu.make_async_remote_copy(
            src_ref=ref, dst_ref=ref, send_sem=b_send.at[n], recv_sem=b_recv.at[n],
            device_id={"col": peer}, device_id_type=MESH,
        )

    b_out = (
        b_copy(0, col, 0, bdepth, xs[0]),
        b_copy(1, col, 0, bdepth, xs[1]),
        b_copy(2, xs[1], 0, hb, xs[0]),
        b_copy(3, xs[0], hb, hb, xs[1]),
        b_copy(4, col, 0, bdepth, sib),
        b_copy(5, xs[1], 0, bdepth, sib),
        b_copy(6, xs[0], 0, bdepth, sib),
        b_copy(7, opp, 0, bdepth, sib),
    )
    other = 1 - 2 * core
    b_in = (
        b_copy(0, xs[1], 0, bdepth, xs[0]),
        b_copy(1, xs[0], 0, bdepth, xs[1]),
        b_copy(2, opp, 0, hb, xs[0]),
        b_copy(3, opp, hb, hb, xs[1]),
        b_copy(4, sib, 0, bdepth, sib),
        b_copy(5, xs[1] + other, 0, bdepth, sib),
        b_copy(6, xs[0] + other, 0, bdepth, sib),
        b_copy(7, opp + other, 0, bdepth, sib),
    )

    def c_copy(q):
        target, d = group_of(q)
        return pltpu.make_async_remote_copy(
            src_ref=acc.at[q], dst_ref=got.at[q], send_sem=c_send.at[q], recv_sem=c_recv.at[q],
            device_id={"layer": target}, device_id_type=MESH,
        )

    def b_of(source):
        return bf[pl.ds(pl.multiple_of(source * depth, depth), depth), :]

    def dot(a, b):
        return jnp.dot(a, b, preferred_element_type=jnp.float32)

    def work(q, h):
        @pl.when(h == 0)
        def _():
            acc[q] = dot(am[pl.ds(pl.multiple_of(q * grp, grp), grp), :], b_of(z))
        @pl.when((h > 0) & (h < half))
        def _():
            at = pl.ds(pl.multiple_of(q * grp, grp), grp)
            n = jnp.maximum(h - 1, 0)
            acc[q] += dot(g[0, n, at, :], b_of(wrap(z - h, nz))) + dot(g[1, n, at, :], b_of(wrap(z + h, nz)))
        @pl.when(h == half)
        def _():
            source = b_of(wrap(z + half, nz))
            for s in range(2):
                at = pl.ds(pl.multiple_of(q * grp + s * sub, sub), sub)
                to = pl.ds(s * sub, sub)
                acc[q, to, :] += dot(g[s, half - 1, at, :], source)

    def settle(q):
        for s in range(2):
            hop(s, q, s, half)[1].wait_recv()

    def step(t, _):
        q, h = t // half, lax.rem(t, half) + 1
        for s in range(2):
            for way in range(2):
                @pl.when(h > 1)
                def _():
                    hop(way, q, s, jnp.maximum(h - 1, 1))[1].wait_recv()
                if way == s:
                    start_hop(way, q, s, h)
                else:
                    @pl.when(h < half)
                    def _():
                        start_hop(way, q, s, h)

        @pl.when(t == 0)
        def _():
            for n in (0, 1, 4):
                b_out[n].start()

        @pl.when((q == 0) & (h == 6))
        def _():
            for n in (0, 1):
                b_in[n].wait_recv()
            for n in (2, 3, 5, 6):
                b_out[n].start()

        @pl.when((q >= 1) & (h == 1))
        def _():
            settle(q - 1)

        @pl.when((q == 1) & (h == 1))
        def _():
            for n in (2, 3):
                b_in[n].wait_recv()
            b_out[7].start()
            for n in range(4, 8):
                b_in[n].wait_recv()

        @pl.when(q >= 1)
        def _():
            @pl.when((h == 1) & (q >= 2))
            def _():
                work(q - 1, half)
                c_copy(q - 1).start()
            work(q, h - 1)

        @pl.when(q == 1)
        def _():
            work(0, h - 1)
            @pl.when(h == half)
            def _():
                work(0, half)
                c_copy(0).start()
        return 0

    lax.fori_loop(0, ny * half, step, 0)
    last = ny - 1
    settle(last)
    work(last, half)
    for q in range(last):
        c_copy(q).wait_recv()
    for r in range(nb):
        at = pl.ds(r * BLK, BLK)
        for p in range(ncols // (2 * BLK)):
            ls = slice(p * 2 * BLK, (p + 1) * 2 * BLK)
            row = y * nb + r
            total = acc[last, at, ls] + got[0, at, ls] + got[1, at, ls] + got[2, at, ls]
            out_ref[at, ls] = total * pair(c_mask[row, 2 * p], c_mask[row, 2 * p + 1])

    def sent(t, _):
        q, h = t // half, lax.rem(t, half) + 1
        for s in range(2):
            for way in range(2):
                if way == s:
                    hop(way, q, s, h)[1].wait_send()
                else:
                    @pl.when(h < half)
                    def _():
                        hop(way, q, s, h)[1].wait_send()
        return 0
    lax.fori_loop(0, ny * half, sent, 0)
    for copy in b_out:
        copy.wait_send()
    for q in range(last):
        c_copy(q).wait_send()


def span(q, s):
    return sum(map(sum, TILES[:q])) + sum(TILES[q][:s]), TILES[q][s]


def compact_kernel(
    nz, nx, ny,
    a_mask_hbm, b_mask_hbm, c_mask_hbm, a_hbm, b_hbm, out_ref, flag_ref,
    a_mask, b_mask, c_mask, a_ref, b_ref, a_tiles, codes_v, codes, places_v, places,
    ring, table, bf, staged, wide, acc, far, got, flags, flag_in,
    in_sem, t_send, t_recv, a_send, a_recv, b_send, b_recv, c_send, c_recv, f_send, f_recv,
):
    z, col, y = lax.axis_index("row"), lax.axis_index("col"), lax.axis_index("layer")
    x, core = col // 2, lax.rem(col, 2)
    half = nz // 2
    rows, depth = a_ref.shape
    bdepth, ncols = b_ref.shape
    grp = rows // ny
    nb = grp // BLK
    nk = depth // BLK

    loads = [
        pltpu.make_async_copy(src, dst, in_sem.at[n])
        for n, (src, dst) in enumerate(
            ((a_mask_hbm, a_mask), (a_hbm, a_ref), (b_mask_hbm, b_mask), (b_hbm, b_ref), (c_mask_hbm, c_mask))
        )
    ]
    for load in loads:
        load.start()

    zs = (wrap(z + 1, nz), wrap(z - 1, nz))
    ys = (wrap(y + 1, ny), wrap(y - 1, ny))
    xs = (wrap(x + 1, nx) * 2 + core, wrap(x - 1, nx) * 2 + core)
    sib = x * 2 + 1 - core
    opp = wrap(x + 2, nx) * 2 + core

    barrier = pltpu.get_barrier_semaphore()
    for axis, peers in (("row", zs), ("col", xs + (sib,)), ("layer", ys)):
        for peer in peers:
            pl.semaphore_signal(barrier, inc=1, device_id={axis: peer}, device_id_type=MESH)

    lane = lax.broadcasted_iota(jnp.int32, (1, 2 * BLK), 1)

    def pair(m0, m1):
        return jnp.where(lane < BLK, m0, m1).astype(jnp.float32)

    def listed(n):
        q, i = n // nb, lax.rem(n, nb)
        low = i < nb // 2
        d = jnp.where(q == 0, 2, jnp.where(q == 3, 0, jnp.where(low, 1, 3)))
        r = jnp.where(q == 1, lax.rem(i, nb // 2), jnp.where(q == 2, nb // 2 + lax.rem(i, nb // 2), i))
        return wrap(y + d, ny) * nb + r

    loads[0].wait()

    def listing(t, carry):
        run, tile, side, bad, order, shift, place = carry
        n, k = t // nk, lax.rem(t, nk)
        row = listed(n)
        m = a_mask[row, k]
        order = jnp.where(lane == run, row * (nk // 2) + k // 2, order)
        shift = jnp.where(lane == run, lax.rem(k, 2), shift)
        place = jnp.where(lane == t, jnp.minimum(tile, NTILES - 1), place)
        place = jnp.where(lane == t + BLK, m * (1 + side), place)
        run, tile, side = run + m, tile + m * side, side + m - 2 * m * side
        q = n // nb
        most = jnp.where(q == 0, UPTO[0], jnp.where(q == 1, UPTO[1], jnp.where(q == 2, UPTO[2], UPTO[3]))) * 2
        bad = jnp.where(run > most, 1, bad)
        return run, tile, side, bad, order, shift, place

    nothing = jnp.zeros((1, 2 * BLK), jnp.int32)
    _, _, _, bad, order, shift, place = lax.fori_loop(
        0, rows // BLK * nk, listing, (0, 0, 0, 0, nothing, nothing, nothing)
    )
    sub8 = lax.broadcasted_iota(jnp.int32, (8, 2 * BLK), 0)
    codes_v[...] = jnp.where(sub8 == 0, order, shift)
    table[0] = jnp.where(sub8 == 0, place, bad)
    to_smem = pltpu.make_async_copy(codes_v, codes, in_sem.at[5])
    to_smem.start()
    loads[1].wait()

    def tiled(row, _):
        for p in range(nk // 2):
            a_tiles[row * (nk // 2) + p] = a_ref[
                pl.ds(pl.multiple_of(row * BLK, BLK), BLK), p * 2 * BLK : (p + 1) * 2 * BLK
            ]
        return 0

    lax.fori_loop(0, rows // BLK, tiled, 0, unroll=4)
    to_smem.wait()

    lanes = lax.broadcasted_iota(jnp.int32, (BLK, 2 * BLK), 1)

    def side_by_side(left, right, stay):
        kept = jnp.where(lanes < BLK, left, right)
        moved = pltpu.roll(jnp.where(lanes < BLK, right, left), BLK, 1)
        return jnp.where(stay == 1, kept, moved)

    def pack(u, _):
        left, right = (a_tiles[codes[0, 2 * u + side]] for side in range(2))
        stay = jnp.where(lanes < BLK, 1 - codes[1, 2 * u], codes[1, 2 * u + 1])
        ring[0, u] = side_by_side(left, right, stay)
        return 0

    lax.fori_loop(0, UPTO[0], pack, 0, unroll=4)

    def slot(way, h):
        return jnp.where((h == 0) | (h == half), h, half * way + h)

    def hop(way, q, s, h):
        first, size = span(q, s)
        return pltpu.make_async_remote_copy(
            src_ref=ring.at[slot(way, h - 1), pl.ds(first, size)],
            dst_ref=ring.at[slot(way, h), pl.ds(first, size)],
            send_sem=a_send.at[way, q, s, h - 1], recv_sem=a_recv.at[way, q, s, h - 1],
            device_id={"row": zs[way]}, device_id_type=MESH,
        )

    def table_hop(way, h):
        return pltpu.make_async_remote_copy(
            src_ref=table.at[slot(way, h - 1)], dst_ref=table.at[slot(way, h)],
            send_sem=t_send.at[way, h - 1], recv_sem=t_recv.at[way, h - 1],
            device_id={"row": zs[way]}, device_id_type=MESH,
        )

    def b_rows(owner, first, count):
        return bf.at[pl.ds(pl.multiple_of(owner * bdepth + first, count), count)]

    hb = bdepth // 2

    def b_copy(n, owner, first, count, peer):
        ref = b_rows(owner, first, count)
        return pltpu.make_async_remote_copy(
            src_ref=ref, dst_ref=ref, send_sem=b_send.at[n], recv_sem=b_recv.at[n],
            device_id={"col": peer}, device_id_type=MESH,
        )

    b_out = (
        b_copy(0, col, 0, bdepth, xs[0]),
        b_copy(1, col, 0, bdepth, xs[1]),
        b_copy(2, xs[1], 0, hb, xs[0]),
        b_copy(3, xs[0], hb, hb, xs[1]),
        b_copy(4, col, 0, bdepth, sib),
        b_copy(5, xs[1], 0, bdepth, sib),
        b_copy(6, xs[0], 0, bdepth, sib),
        b_copy(7, opp, 0, bdepth, sib),
    )
    other = 1 - 2 * core
    b_in = (
        b_copy(0, xs[1], 0, bdepth, xs[0]),
        b_copy(1, xs[0], 0, bdepth, xs[1]),
        b_copy(2, opp, 0, hb, xs[0]),
        b_copy(3, opp, hb, hb, xs[1]),
        b_copy(4, sib, 0, bdepth, sib),
        b_copy(5, xs[1] + other, 0, bdepth, sib),
        b_copy(6, xs[0] + other, 0, bdepth, sib),
        b_copy(7, opp + other, 0, bdepth, sib),
    )

    def mask_b(t, _):
        at = pl.ds(pl.multiple_of(t * BLK, BLK), BLK)
        to = pl.ds(pl.multiple_of(col * bdepth + t * BLK, BLK), BLK)
        for p in range(ncols // (2 * BLK)):
            ls = slice(p * 2 * BLK, (p + 1) * 2 * BLK)
            m = pair(b_mask[t, 2 * p], b_mask[t, 2 * p + 1]).astype(bf.dtype)
            bf[to, ls] = b_ref[at, ls] * m
        return 0

    hg = grp // 2

    def c_copy(q, way):
        return pltpu.make_async_remote_copy(
            src_ref=acc.at[q, pl.ds(way * hg, hg)],
            dst_ref=far.at[way] if q == 0 else got.at[way, q - 1],
            send_sem=c_send.at[way, q], recv_sem=c_recv.at[way, q],
            device_id={"layer": ys[way]}, device_id_type=MESH,
        )

    rounds = (("col", xs), ("col", xs), ("col", (sib,)), ("layer", ys), ("layer", ys))

    def f_copy(n, m):
        axis, peers = rounds[n]
        return pltpu.make_async_remote_copy(
            src_ref=flags.at[n], dst_ref=flag_in.at[n, m], send_sem=f_send.at[n, m], recv_sem=f_recv.at[n, m],
            device_id={axis: peers[m]}, device_id_type=MESH,
        )

    def f_take(n):
        value = flags[n]
        for m in range(len(rounds[n][1])):
            f_copy(n, m).wait_recv()
            value = jnp.maximum(value, flag_in[n, m])
        return value

    def settle(q):
        for s in range(2):
            hop(s, q, s, half).wait_recv()

    def table_step(h):
        for way in range(2):
            @pl.when(h > 1)
            def _():
                table_hop(way, jnp.maximum(h - 1, 1)).wait_recv()
            if way == 0:
                table_hop(way, h).start()
            else:
                @pl.when(h < half)
                def _():
                    table_hop(way, jnp.minimum(h, half - 1)).start()

    def lanes_step(q, h, phases):
        for qi in phases:
            @pl.when(q == qi)
            def _():
                for s in range(2):
                    for way in range(2):
                        @pl.when(h > 1)
                        def _():
                            hop(way, qi, s, jnp.maximum(h - 1, 1)).wait_recv()
                        if way == s:
                            hop(way, qi, s, h).start()
                        else:
                            @pl.when(h < half)
                            def _():
                                hop(way, qi, s, jnp.minimum(h, half - 1)).start()

    def b_of(source):
        return bf[pl.ds(pl.multiple_of(source * depth, depth), depth), :]

    def work(q, w):
        for qi in range(4):
            @pl.when(q == qi)
            def _():
                size = UPTO[qi]
                for j in range(2):
                    staged[j, 0:size] = ring[w + half * j, 0:size]
        for i in range(nb):
            for j in range(2):
                for p in range(nk // 2):
                    here, t = w + half * j, q * (nb * nk) + i * nk + 2 * p
                    left, right = (staged[j, places[here, t + side]] for side in range(2))
                    at_left, at_right = places[here, t + BLK], places[here, t + 1 + BLK]
                    stay = jnp.where(lanes < BLK, at_left, at_right - 1)
                    keep = pair(jnp.minimum(at_left, 1), jnp.minimum(at_right, 1)).astype(wide.dtype)
                    to = (2 * j + p) * 2 * BLK
                    wide[i * BLK : (i + 1) * BLK, to : to + 2 * BLK] = side_by_side(left, right, stay) * keep
        second = jnp.where(w == 0, z + half, z + w)
        acc[q] += jnp.dot(
            wide[:, :depth], b_of(wrap(z - w, nz)), preferred_element_type=jnp.float32
        ) + jnp.dot(wide[:, depth:], b_of(wrap(second, nz)), preferred_element_type=jnp.float32)

    def zero(t, _):
        acc[t // 4, pl.ds(pl.multiple_of(lax.rem(t, 4) * BLK, BLK), BLK), :] = jnp.zeros((BLK, ncols), jnp.float32)
        return 0

    pl.semaphore_wait(barrier, 7)

    def step(r, _):
        xq, xh = 2 * (r // half), lax.rem(r, half) + 1
        yq, yh = 2 * ((r + half - 1) // half) - 1, lax.rem(r + half - 1, half) + 1

        @pl.when(r < half)
        def _():
            table_step(r + 1)

        @pl.when(r < 2 * half)
        def _():
            lanes_step(xq, xh, (0, 2))

        @pl.when(r == 0)
        def _():
            lax.fori_loop(UPTO[0], NTILES, pack, 0, unroll=2)

        @pl.when(r > 0)
        def _():
            lanes_step(yq, yh, (1, 3))

        @pl.when(r == 0)
        def _():
            for load in loads[2:]:
                load.wait()
            lax.fori_loop(0, bdepth // BLK, mask_b, 0)
            for n in (0, 1, 4):
                b_out[n].start()
            lax.fori_loop(0, 16, zero, 0)

        @pl.when(r == 3)
        def _():
            for n in (0, 1):
                b_in[n].wait_recv()
            for n in (2, 3, 5, 6):
                b_out[n].start()

        @pl.when(r == 5)
        def _():
            for n in (2, 3):
                b_in[n].wait_recv()
            b_out[7].start()

        @pl.when(r == half)
        def _():
            for n in range(4, 8):
                b_in[n].wait_recv()
            settle(0)
            table_hop(0, half).wait_recv()

            def row(j, over):
                one = table[j]
                places_v[pl.ds(j, 1), :] = one[0:1, :]
                return jnp.maximum(over, one)

            flags[0] = lax.fori_loop(0, nz, row, jnp.zeros((8, 2 * BLK), jnp.int32))
            down = pltpu.make_async_copy(places_v, places, in_sem.at[6])
            down.start()
            down.wait()

        @pl.when(r == half + 1)
        def _():
            settle(1)

        for n in range(len(rounds)):
            @pl.when(r == half + 1 + n)
            def _():
                if n:
                    flags[n] = f_take(n - 1)
                for m in range(len(rounds[n][1])):
                    f_copy(n, m).start()

        @pl.when(r == 2 * half)
        def _():
            settle(2)

        def items(q, first, last):
            def one(w, _):
                work(q, lax.rem(w, half))
                return 0
            lax.fori_loop(first, last, one, 0)

        late = r - half - 4
        q = jnp.where(r < half + 2, 0, jnp.where(r < half + 4, 1, 2))
        first = jnp.where(r < half + 4, 1 + lax.rem(r, 2) * 4, 2 * late + 1)
        last = jnp.where(r < half, first, jnp.where(r < half + 4, first + 4, jnp.where(r < 2 * half, jnp.minimum(first + 2, half), half + 1)))
        first = jnp.where(r == 2 * half, half, first)
        items(q, first, last)

        @pl.when(r == half + 1)
        def _():
            for way in range(2):
                c_copy(0, way).start()

        @pl.when(r == half + 4)
        def _():
            c_copy(0, 0).wait_recv()
            acc[1, 0:hg, :] += far[0]
            for way in range(2):
                c_copy(1, way).start()

        @pl.when(r == 2 * half)
        def _():
            c_copy(0, 1).wait_recv()
            acc[2, hg:, :] += far[1]
            for way in range(2):
                c_copy(2, way).start()

        own = 2 * (r - half - 5) + 1
        items(3, own, jnp.where(r < half + 5, own, jnp.minimum(own + 2, half)))
        return 0

    lax.fori_loop(0, 2 * half + 1, step, 0)
    settle(3)
    work(3, 0)
    for q in (1, 2):
        for way in range(2):
            c_copy(q, way).wait_recv()
    for r in range(nb):
        at = pl.ds(r * BLK, BLK)
        part, sub = r // (nb // 2), pl.ds(r % (nb // 2) * BLK, BLK)
        for p in range(ncols // (2 * BLK)):
            ls = slice(p * 2 * BLK, (p + 1) * 2 * BLK)
            row = y * nb + r
            total = acc[3, at, ls] + got[0, part, sub, ls] + got[1, part, sub, ls]
            out_ref[at, ls] = total * pair(c_mask[row, 2 * p], c_mask[row, 2 * p + 1])
    flag_ref[...] = f_take(len(rounds) - 1)

    def sent(t, _):
        h = t + 1
        table_hop(0, h).wait_send()

        @pl.when(h < half)
        def _():
            table_hop(1, jnp.minimum(h, half - 1)).wait_send()

        for q in range(4):
            for s in range(2):
                for way in range(2):
                    if way == s:
                        hop(way, q, s, h).wait_send()
                    else:
                        @pl.when(h < half)
                        def _():
                            hop(way, q, s, jnp.minimum(h, half - 1)).wait_send()
        return 0

    lax.fori_loop(0, half, sent, 0)
    for copy in b_out:
        copy.wait_send()
    for q in range(3):
        for way in range(2):
            c_copy(q, way).wait_send()
    for n in range(len(rounds)):
        for m in range(len(rounds[n][1])):
            f_copy(n, m).wait_send()


def dense(nz, nx, ny, a_blocks, a_mask, b_blocks, b_mask, c_mask):
    rows, depth = a_blocks.shape
    bdepth, ncols = b_blocks.shape
    grp = rows // ny
    half = nz // 2
    vmem, smem = pl.BlockSpec(memory_space=pltpu.VMEM), pl.BlockSpec(memory_space=pltpu.SMEM)
    dma = pltpu.SemaphoreType.DMA
    return pl.pallas_call(
        functools.partial(dense_kernel, nz, nx, ny),
        out_shape=jax.ShapeDtypeStruct((grp, ncols), jnp.float32),
        in_specs=[smem, smem, smem, vmem, vmem],
        out_specs=vmem,
        scratch_shapes=[
            pltpu.VMEM((rows, depth), jnp.bfloat16),
            pltpu.VMEM((2, half, rows, depth), jnp.bfloat16),
            pltpu.VMEM((2 * nx * bdepth, ncols), jnp.bfloat16),
            pltpu.VMEM((ny, grp, ncols), jnp.float32),
            pltpu.VMEM((ny - 1, grp, ncols), jnp.float32),
            dma((2, ny, 2, half)),
            dma((2, ny, 2, half)),
            dma((8,)),
            dma((8,)),
            dma((ny - 1,)),
            dma((ny - 1,)),
        ],
        compiler_params=pltpu.CompilerParams(
            collective_id=1, has_side_effects=True, vmem_limit_bytes=40 * 2**20
        ),
    )(a_mask, b_mask, c_mask, a_blocks, b_blocks)


def compact(nz, nx, ny, a_blocks, a_mask, b_blocks, b_mask, c_mask):
    rows, depth = a_blocks.shape
    bdepth, ncols = b_blocks.shape
    grp = rows // ny
    half = nz // 2
    vmem, anywhere = pl.BlockSpec(memory_space=pltpu.VMEM), pl.BlockSpec(memory_space=pl.ANY)
    dma = pltpu.SemaphoreType.DMA
    return pl.pallas_call(
        functools.partial(compact_kernel, nz, nx, ny),
        out_shape=(
            jax.ShapeDtypeStruct((grp, ncols), jnp.float32),
            jax.ShapeDtypeStruct((8, 128), jnp.int32),
        ),
        in_specs=[anywhere] * 5,
        out_specs=(vmem, vmem),
        scratch_shapes=[
            pltpu.SMEM(a_mask.shape, jnp.int32),
            pltpu.SMEM(b_mask.shape, jnp.int32),
            pltpu.SMEM(c_mask.shape, jnp.int32),
            pltpu.VMEM((rows, depth), jnp.bfloat16),
            pltpu.VMEM((bdepth, ncols), jnp.bfloat16),
            pltpu.VMEM((rows * depth // (2 * BLK * BLK), BLK, 2 * BLK), jnp.bfloat16),
            pltpu.VMEM((8, 128), jnp.int32),
            pltpu.SMEM((8, 128), jnp.int32),
            pltpu.VMEM((nz, 128), jnp.int32),
            pltpu.SMEM((nz, 128), jnp.int32),
            pltpu.VMEM((nz, NTILES, BLK, 2 * BLK), jnp.bfloat16),
            pltpu.VMEM((nz, 8, 128), jnp.int32),
            pltpu.VMEM((2 * nx * bdepth, ncols), jnp.bfloat16),
            pltpu.VMEM((2, NTILES, BLK, 2 * BLK), jnp.bfloat16),
            pltpu.VMEM((grp, 2 * depth), jnp.bfloat16),
            pltpu.VMEM((ny, grp, ncols), jnp.float32),
            pltpu.VMEM((2, grp // 2, ncols), jnp.float32),
            pltpu.VMEM((2, 2, grp // 2, ncols), jnp.float32),
            pltpu.VMEM((5, 8, 128), jnp.int32),
            pltpu.VMEM((5, 2, 8, 128), jnp.int32),
            dma((7,)),
            dma((2, half)),
            dma((2, half)),
            dma((2, 4, 2, half)),
            dma((2, 4, 2, half)),
            dma((8,)),
            dma((8,)),
            dma((2, 3)),
            dma((2, 3)),
            dma((5, 2)),
            dma((5, 2)),
        ],
        compiler_params=pltpu.CompilerParams(
            collective_id=0, has_side_effects=True, vmem_limit_bytes=40 * 2**20
        ),
    )(a_mask, b_mask, c_mask, a_blocks, b_blocks)


def shards(nz, nx, ny, *args):
    product, flag = compact(nz, nx, ny, *args)
    return lax.cond(flag[1, 0] > 0, lambda: dense(nz, nx, ny, *args), lambda: product)


def solution(mesh):
    nz, ncol, ny = mesh.shape["row"], mesh.shape["col"], mesh.shape["layer"]
    in_specs = (
        P("col", ("layer", "row")),
        P("col", ("layer", "row")),
        P(("layer", "col"), "row"),
        P(("layer", "col"), "row"),
        P("col", "row"),
    )
    out_specs = P(("col", "layer"), "row")
    body = functools.partial(shards, nz, ncol // 2, ny)
    return jax.shard_map(body, mesh=mesh, in_specs=in_specs, out_specs=out_specs, check_vma=False)
```

```python
import functools

import jax
import jax.numpy as jnp
from jax import lax
from jax.experimental import pallas as pl
from jax.experimental.pallas import tpu as pltpu
from jax.sharding import PartitionSpec as P

BLK = 64
MESH = pl.DeviceIdType.MESH
ORDER = (1, 3, 2, 0)

TILES = ((4, 4), (4, 4), (3, 2), (3, 2))
NTILES = sum(map(sum, TILES))
UPTO = tuple(sum(map(sum, TILES[: q + 1])) for q in range(4))

READY = 24

HOPS = (
    0, 3, 1, 0, 3, 1, 0, 2, 3, 1, 0, 2, 3, 1, 0, 2, 3, 1, 0, 4, 2, 3, 1, 0, 5, 4, 2, 3, 1, 0,
    5, 4, 6, 2, 5, 4, 7, 6, 2, 5, 4, 7, 6, 2, 5, 4, 7, 6, 5, 4, 7, 6, 5, 4, 7, 6, 7, 6, 7, 6,
)


def plan(half):
    taken, hops, settled, jobs, sends = [0] * 8, [], [], [], []
    done, worked = set(), set()
    last = [max(i for i, chunk in enumerate(HOPS) if chunk // 2 == q) for q in range(4)]
    todo = [(q, w % half) for q in range(4) for w in range(1, half + 1)]
    i = 0
    while len(worked) < len(todo):
        hops.append(None)
        if i < len(HOPS):
            chunk = HOPS[i]
            taken[chunk] += 1
            hops[i] = (chunk // 2, chunk % 2, taken[chunk])
        settled.append([q for q in range(4) if q not in done and i >= min(last[q] + 2, len(HOPS) + (q == 3))])
        done.update(settled[i])
        arrived = [half if q in done else min(taken[2 * q], taken[2 * q + 1]) - 1 for q in range(4)]
        job = -1
        for q, w in todo:
            if (
                i >= READY
                and (q, w) not in worked
                and (w or half) <= arrived[q]
                and (q == 0 or (q - 1, w) in worked)
            ):
                job = q * half + w
                worked.add((q, w))
                break
        jobs.append(job)
        for q in range(3):
            if len(sends) == q and all((q, w) in worked for w in range(half)):
                sends.append(max(i, sends[-1] + 3) if sends else i)
        i += 1
    return hops, settled, jobs, sends


def wrap(value, size):
    return lax.rem(value + size, size)


def dense_kernel(
    nz, nx, ny,
    a_mask, b_mask, c_mask, a_ref, b_ref, out_ref,
    am, g, bf, acc, got,
    a_send, a_recv, b_send, b_recv, c_send, c_recv,
):
    z, col, y = lax.axis_index("row"), lax.axis_index("col"), lax.axis_index("layer")
    x, core = col // 2, lax.rem(col, 2)
    half = nz // 2
    rows, depth = a_ref.shape
    grp = rows // ny
    sub = grp // 2
    bdepth, ncols = b_ref.shape

    zs = (wrap(z + 1, nz), wrap(z - 1, nz))
    xs = (wrap(x + 1, nx) * 2 + core, wrap(x - 1, nx) * 2 + core)
    sib = x * 2 + 1 - core
    opp = wrap(x + 2, nx) * 2 + core

    barrier = pltpu.get_barrier_semaphore()
    for peer in zs:
        pl.semaphore_signal(barrier, inc=1, device_id={"row": peer}, device_id_type=MESH)
    for peer in xs + (sib,):
        pl.semaphore_signal(barrier, inc=1, device_id={"col": peer}, device_id_type=MESH)
    for d in range(1, ny):
        pl.semaphore_signal(barrier, inc=1, device_id={"layer": wrap(y + d, ny)}, device_id_type=MESH)

    lane = lax.broadcasted_iota(jnp.int32, (1, 2 * BLK), 1)

    def pair(m0, m1):
        return jnp.where(lane < BLK, m0, m1).astype(jnp.float32)

    def group_of(q):
        d = jnp.where(q == 0, ORDER[0], jnp.where(q == 1, ORDER[1], jnp.where(q == 2, ORDER[2], 0)))
        return wrap(y + d, ny), d

    nb = grp // BLK
    def mask_a(t, _):
        q, r = t // nb, lax.rem(t, nb)
        src = group_of(q)[0] * nb + r
        at = pl.ds(pl.multiple_of(src * BLK, BLK), BLK)
        to = pl.ds(pl.multiple_of(t * BLK, BLK), BLK)
        for p in range(depth // (2 * BLK)):
            ls = slice(p * 2 * BLK, (p + 1) * 2 * BLK)
            m = pair(a_mask[src, 2 * p], a_mask[src, 2 * p + 1]).astype(am.dtype)
            am[to, ls] = a_ref[at, ls] * m
        return 0
    lax.fori_loop(0, rows // BLK, mask_a, 0)

    def mask_b(t, _):
        at = pl.ds(pl.multiple_of(t * BLK, BLK), BLK)
        to = pl.ds(pl.multiple_of(col * bdepth + t * BLK, BLK), BLK)
        for p in range(ncols // (2 * BLK)):
            ls = slice(p * 2 * BLK, (p + 1) * 2 * BLK)
            m = pair(b_mask[t, 2 * p], b_mask[t, 2 * p + 1]).astype(bf.dtype)
            bf[to, ls] = b_ref[at, ls] * m
        return 0
    lax.fori_loop(0, bdepth // BLK, mask_b, 0)

    pl.semaphore_wait(barrier, 5 + ny - 1)

    def chunk(ref, q, s):
        return ref.at[pl.ds(pl.multiple_of(q * grp + s * sub, sub), sub)]

    def hop(way, q, s, h):
        dst = chunk(g.at[way, h - 1], q, s)
        return dst, pltpu.make_async_remote_copy(
            src_ref=dst, dst_ref=dst,
            send_sem=a_send.at[way, q, s, h - 1], recv_sem=a_recv.at[way, q, s, h - 1],
            device_id={"row": zs[way]}, device_id_type=MESH,
        )

    def start_hop(way, q, s, h):
        dst = chunk(g.at[way, h - 1], q, s)
        def go(src):
            pltpu.make_async_remote_copy(
                src_ref=src, dst_ref=dst,
                send_sem=a_send.at[way, q, s, h - 1], recv_sem=a_recv.at[way, q, s, h - 1],
                device_id={"row": zs[way]}, device_id_type=MESH,
            ).start()
        @pl.when(h == 1)
        def _():
            go(chunk(am, q, s))
        @pl.when(h > 1)
        def _():
            go(chunk(g.at[way, jnp.maximum(h - 2, 0)], q, s))

    def b_rows(owner, first, count):
        return bf.at[pl.ds(pl.multiple_of(owner * bdepth + first, count), count)]

    hb = bdepth // 2
    def b_copy(n, owner, first, count, peer):
        ref = b_rows(owner, first, count)
        return pltpu.make_async_remote_copy(
            src_ref=ref, dst_ref=ref, send_sem=b_send.at[n], recv_sem=b_recv.at[n],
            device_id={"col": peer}, device_id_type=MESH,
        )

    b_out = (
        b_copy(0, col, 0, bdepth, xs[0]),
        b_copy(1, col, 0, bdepth, xs[1]),
        b_copy(2, xs[1], 0, hb, xs[0]),
        b_copy(3, xs[0], hb, hb, xs[1]),
        b_copy(4, col, 0, bdepth, sib),
        b_copy(5, xs[1], 0, bdepth, sib),
        b_copy(6, xs[0], 0, bdepth, sib),
        b_copy(7, opp, 0, bdepth, sib),
    )
    other = 1 - 2 * core
    b_in = (
        b_copy(0, xs[1], 0, bdepth, xs[0]),
        b_copy(1, xs[0], 0, bdepth, xs[1]),
        b_copy(2, opp, 0, hb, xs[0]),
        b_copy(3, opp, hb, hb, xs[1]),
        b_copy(4, sib, 0, bdepth, sib),
        b_copy(5, xs[1] + other, 0, bdepth, sib),
        b_copy(6, xs[0] + other, 0, bdepth, sib),
        b_copy(7, opp + other, 0, bdepth, sib),
    )

    def c_copy(q):
        target, d = group_of(q)
        return pltpu.make_async_remote_copy(
            src_ref=acc.at[q], dst_ref=got.at[q], send_sem=c_send.at[q], recv_sem=c_recv.at[q],
            device_id={"layer": target}, device_id_type=MESH,
        )

    def b_of(source):
        return bf[pl.ds(pl.multiple_of(source * depth, depth), depth), :]

    def dot(a, b):
        return jnp.dot(a, b, preferred_element_type=jnp.float32)

    def work(q, h):
        @pl.when(h == 0)
        def _():
            acc[q] = dot(am[pl.ds(pl.multiple_of(q * grp, grp), grp), :], b_of(z))
        @pl.when((h > 0) & (h < half))
        def _():
            at = pl.ds(pl.multiple_of(q * grp, grp), grp)
            n = jnp.maximum(h - 1, 0)
            acc[q] += dot(g[0, n, at, :], b_of(wrap(z - h, nz))) + dot(g[1, n, at, :], b_of(wrap(z + h, nz)))
        @pl.when(h == half)
        def _():
            source = b_of(wrap(z + half, nz))
            for s in range(2):
                at = pl.ds(pl.multiple_of(q * grp + s * sub, sub), sub)
                to = pl.ds(s * sub, sub)
                acc[q, to, :] += dot(g[s, half - 1, at, :], source)

    def settle(q):
        for s in range(2):
            hop(s, q, s, half)[1].wait_recv()

    def step(t, _):
        q, h = t // half, lax.rem(t, half) + 1
        for s in range(2):
            for way in range(2):
                @pl.when(h > 1)
                def _():
                    hop(way, q, s, jnp.maximum(h - 1, 1))[1].wait_recv()
                if way == s:
                    start_hop(way, q, s, h)
                else:
                    @pl.when(h < half)
                    def _():
                        start_hop(way, q, s, h)

        @pl.when(t == 0)
        def _():
            for n in (0, 1, 4):
                b_out[n].start()

        @pl.when((q == 0) & (h == 6))
        def _():
            for n in (0, 1):
                b_in[n].wait_recv()
            for n in (2, 3, 5, 6):
                b_out[n].start()

        @pl.when((q >= 1) & (h == 1))
        def _():
            settle(q - 1)

        @pl.when((q == 1) & (h == 1))
        def _():
            for n in (2, 3):
                b_in[n].wait_recv()
            b_out[7].start()
            for n in range(4, 8):
                b_in[n].wait_recv()

        @pl.when(q >= 1)
        def _():
            @pl.when((h == 1) & (q >= 2))
            def _():
                work(q - 1, half)
                c_copy(q - 1).start()
            work(q, h - 1)

        @pl.when(q == 1)
        def _():
            work(0, h - 1)
            @pl.when(h == half)
            def _():
                work(0, half)
                c_copy(0).start()
        return 0

    lax.fori_loop(0, ny * half, step, 0)
    last = ny - 1
    settle(last)
    work(last, half)
    for q in range(last):
        c_copy(q).wait_recv()
    for r in range(nb):
        at = pl.ds(r * BLK, BLK)
        for p in range(ncols // (2 * BLK)):
            ls = slice(p * 2 * BLK, (p + 1) * 2 * BLK)
            row = y * nb + r
            total = acc[last, at, ls] + got[0, at, ls] + got[1, at, ls] + got[2, at, ls]
            out_ref[at, ls] = total * pair(c_mask[row, 2 * p], c_mask[row, 2 * p + 1])

    def sent(t, _):
        q, h = t // half, lax.rem(t, half) + 1
        for s in range(2):
            for way in range(2):
                if way == s:
                    hop(way, q, s, h)[1].wait_send()
                else:
                    @pl.when(h < half)
                    def _():
                        hop(way, q, s, h)[1].wait_send()
        return 0
    lax.fori_loop(0, ny * half, sent, 0)
    for copy in b_out:
        copy.wait_send()
    for q in range(last):
        c_copy(q).wait_send()


def span(q, s):
    return sum(map(sum, TILES[:q])) + sum(TILES[q][:s]), TILES[q][s]


def compact_kernel(
    nz, nx, ny,
    a_mask_hbm, b_mask_hbm, c_mask_hbm, a_hbm, b_hbm, out_ref, flag_ref,
    a_mask, b_mask, c_mask, a_ref, b_ref, a_tiles, codes_v, codes, places_v, places,
    ring, table, bf, staged, wide, acc, far, got, flags, flag_in,
    in_sem, t_send, t_recv, a_send, a_recv, b_send, b_recv, c_send, c_recv, f_send, f_recv,
):
    z, col, y = lax.axis_index("row"), lax.axis_index("col"), lax.axis_index("layer")
    x, core = col // 2, lax.rem(col, 2)
    half = nz // 2
    rows, depth = a_ref.shape
    bdepth, ncols = b_ref.shape
    grp = rows // ny
    nb = grp // BLK
    nk = depth // BLK

    loads = [
        pltpu.make_async_copy(src, dst, in_sem.at[n])
        for n, (src, dst) in enumerate(
            ((a_mask_hbm, a_mask), (a_hbm, a_ref), (b_mask_hbm, b_mask), (b_hbm, b_ref), (c_mask_hbm, c_mask))
        )
    ]
    for load in loads:
        load.start()

    zs = (wrap(z + 1, nz), wrap(z - 1, nz))
    ys = (wrap(y + 1, ny), wrap(y - 1, ny))
    xs = (wrap(x + 1, nx) * 2 + core, wrap(x - 1, nx) * 2 + core)
    sib = x * 2 + 1 - core
    opp = wrap(x + 2, nx) * 2 + core

    barrier = pltpu.get_barrier_semaphore()
    for axis, peers in (("row", zs), ("col", xs + (sib,)), ("layer", ys)):
        for peer in peers:
            pl.semaphore_signal(barrier, inc=1, device_id={axis: peer}, device_id_type=MESH)

    lane = lax.broadcasted_iota(jnp.int32, (1, 2 * BLK), 1)

    def pair(m0, m1):
        return jnp.where(lane < BLK, m0, m1).astype(jnp.float32)

    def listed(n):
        q, i = n // nb, lax.rem(n, nb)
        low = i < nb // 2
        d = jnp.where(q == 0, 2, jnp.where(q == 3, 0, jnp.where(low, 1, 3)))
        r = jnp.where(q == 1, lax.rem(i, nb // 2), jnp.where(q == 2, nb // 2 + lax.rem(i, nb // 2), i))
        return wrap(y + d, ny) * nb + r

    loads[0].wait()

    def listing(t, carry):
        run, tile, side, bad, order, shift, place = carry
        n, k = t // nk, lax.rem(t, nk)
        row = listed(n)
        m = a_mask[k, row]
        order = jnp.where(lane == run, row * (nk // 2) + k // 2, order)
        shift = jnp.where(lane == run, lax.rem(k, 2), shift)
        place = jnp.where(lane == t, jnp.minimum(tile, NTILES - 1), place)
        place = jnp.where(lane == t + BLK, m * (1 + side), place)
        run, tile, side = run + m, tile + m * side, side + m - 2 * m * side
        q = n // nb
        most = jnp.where(q == 0, UPTO[0], jnp.where(q == 1, UPTO[1], jnp.where(q == 2, UPTO[2], UPTO[3]))) * 2
        bad = jnp.where(run > most, 1, bad)
        return run, tile, side, bad, order, shift, place

    nothing = jnp.zeros((1, 2 * BLK), jnp.int32)
    _, _, _, bad, order, shift, place = lax.fori_loop(
        0, rows // BLK * nk, listing, (0, 0, 0, 0, nothing, nothing, nothing), unroll=8
    )
    sub8 = lax.broadcasted_iota(jnp.int32, (8, 2 * BLK), 0)
    codes_v[...] = jnp.where(sub8 == 0, order, shift)
    table[0] = jnp.where(sub8 == 0, place, bad)
    to_smem = pltpu.make_async_copy(codes_v, codes, in_sem.at[5])
    to_smem.start()
    loads[1].wait()

    def tiled(row, _):
        for p in range(nk // 2):
            a_tiles[row * (nk // 2) + p] = a_ref[
                pl.ds(pl.multiple_of(row * BLK, BLK), BLK), p * 2 * BLK : (p + 1) * 2 * BLK
            ]
        return 0

    lax.fori_loop(0, rows // BLK, tiled, 0, unroll=4)
    to_smem.wait()

    lanes = lax.broadcasted_iota(jnp.int32, (BLK, 2 * BLK), 1)

    def side_by_side(left, right, stay):
        kept = jnp.where(lanes < BLK, left, right)
        moved = pltpu.roll(jnp.where(lanes < BLK, right, left), BLK, 1)
        return jnp.where(stay == 1, kept, moved)

    def pack(u, _):
        left, right = (a_tiles[codes[0, 2 * u + side]] for side in range(2))
        stay = jnp.where(lanes < BLK, 1 - codes[1, 2 * u], codes[1, 2 * u + 1])
        ring[0, u] = side_by_side(left, right, stay)
        return 0

    lax.fori_loop(0, UPTO[0], pack, 0, unroll=4)

    def slot(way, h):
        return h if h in (0, half) else half * way + h

    def hop(way, q, s, h):
        first, size = span(q, s)
        return pltpu.make_async_remote_copy(
            src_ref=ring.at[slot(way, h - 1), pl.ds(first, size)],
            dst_ref=ring.at[slot(way, h), pl.ds(first, size)],
            send_sem=a_send.at[way, q, s, h - 1], recv_sem=a_recv.at[way, q, s, h - 1],
            device_id={"row": zs[way]}, device_id_type=MESH,
        )

    def table_hop(way, h):
        return pltpu.make_async_remote_copy(
            src_ref=table.at[slot(way, h - 1)], dst_ref=table.at[slot(way, h)],
            send_sem=t_send.at[way, h - 1], recv_sem=t_recv.at[way, h - 1],
            device_id={"row": zs[way]}, device_id_type=MESH,
        )

    def b_rows(owner, first, count):
        return bf.at[pl.ds(pl.multiple_of(owner * bdepth + first, count), count)]

    hb = bdepth // 2

    def b_copy(n, owner, first, count, peer):
        ref = b_rows(owner, first, count)
        return pltpu.make_async_remote_copy(
            src_ref=ref, dst_ref=ref, send_sem=b_send.at[n], recv_sem=b_recv.at[n],
            device_id={"col": peer}, device_id_type=MESH,
        )

    b_out = (
        b_copy(0, col, 0, bdepth, xs[0]),
        b_copy(1, col, 0, bdepth, xs[1]),
        b_copy(2, xs[1], 0, hb, xs[0]),
        b_copy(3, xs[0], hb, hb, xs[1]),
        b_copy(4, col, 0, bdepth, sib),
        b_copy(5, xs[1], 0, bdepth, sib),
        b_copy(6, xs[0], 0, bdepth, sib),
        b_copy(7, opp, 0, bdepth, sib),
    )
    other = 1 - 2 * core
    b_in = (
        b_copy(0, xs[1], 0, bdepth, xs[0]),
        b_copy(1, xs[0], 0, bdepth, xs[1]),
        b_copy(2, opp, 0, hb, xs[0]),
        b_copy(3, opp, hb, hb, xs[1]),
        b_copy(4, sib, 0, bdepth, sib),
        b_copy(5, xs[1] + other, 0, bdepth, sib),
        b_copy(6, xs[0] + other, 0, bdepth, sib),
        b_copy(7, opp + other, 0, bdepth, sib),
    )

    def mask_b(t, _):
        at = pl.ds(pl.multiple_of(t * BLK, BLK), BLK)
        to = pl.ds(pl.multiple_of(col * bdepth + t * BLK, BLK), BLK)
        for p in range(ncols // (2 * BLK)):
            ls = slice(p * 2 * BLK, (p + 1) * 2 * BLK)
            m = pair(b_mask[t, 2 * p], b_mask[t, 2 * p + 1]).astype(bf.dtype)
            bf[to, ls] = b_ref[at, ls] * m
        return 0

    hg = grp // 2

    def c_copy(q, way):
        return pltpu.make_async_remote_copy(
            src_ref=acc.at[q, pl.ds(way * hg, hg)],
            dst_ref=far.at[way] if q == 0 else got.at[way, q - 1],
            send_sem=c_send.at[way, q], recv_sem=c_recv.at[way, q],
            device_id={"layer": ys[way]}, device_id_type=MESH,
        )

    rounds = (("col", xs), ("col", xs), ("col", (sib,)), ("layer", ys), ("layer", ys))

    def f_copy(n, m):
        axis, peers = rounds[n]
        return pltpu.make_async_remote_copy(
            src_ref=flags.at[n], dst_ref=flag_in.at[n, m], send_sem=f_send.at[n, m], recv_sem=f_recv.at[n, m],
            device_id={axis: peers[m]}, device_id_type=MESH,
        )

    def f_take(n):
        value = flags[n]
        for m in range(len(rounds[n][1])):
            f_copy(n, m).wait_recv()
            value = jnp.maximum(value, flag_in[n, m])
        return value

    def settle(q):
        for s in range(2):
            hop(s, q, s, half).wait_recv()
            hop(1 - s, q, s, half - 1).wait_recv()

    def table_step(h):
        for way in range(2):
            if h > 1:
                table_hop(way, h - 1).wait_recv()
            if way == 0 or h < half:
                table_hop(way, h).start()

    def take_hop(q, s, h):
        for way in range(2):
            piece = s if way == 0 else 1 - s
            if h > 1:
                hop(way, q, piece, h - 1).wait_recv()
            hop(way, q, piece, h).start()

    def b_of(source):
        return bf[pl.ds(pl.multiple_of(source * depth, depth), depth), :]

    def work(q, w):
        first, size = span(q, 0)[0], sum(TILES[q])
        for j in range(2):
            staged[w + half * j, first : first + size] = ring[w + half * j, first : first + size]
        for i in range(nb):
            for j in range(2):
                for p in range(nk // 2):
                    here, t = w + half * j, q * (nb * nk) + i * nk + 2 * p
                    left, right = (staged[here, places[here, t + side]] for side in range(2))
                    at_left, at_right = places[here, t + BLK], places[here, t + 1 + BLK]
                    kept = pair(jnp.where(at_left == 1, 1, 0), jnp.where(at_right == 2, 1, 0)).astype(wide.dtype)
                    moved = pair(jnp.where(at_left == 2, 1, 0), jnp.where(at_right == 1, 1, 0)).astype(wide.dtype)
                    to = (2 * j + p) * 2 * BLK
                    wide[i * BLK : (i + 1) * BLK, to : to + 2 * BLK] = (
                        jnp.where(lanes < BLK, left, right) * kept
                        + pltpu.roll(jnp.where(lanes < BLK, right, left), BLK, 1) * moved
                    )
        second = z + (w or half)
        acc[q] += jnp.dot(
            wide[:, :depth], b_of(wrap(z - w, nz)), preferred_element_type=jnp.float32
        ) + jnp.dot(wide[:, depth:], b_of(wrap(second, nz)), preferred_element_type=jnp.float32)

    def zero(t, _):
        acc[t // 4, pl.ds(pl.multiple_of(lax.rem(t, 4) * BLK, BLK), BLK), :] = jnp.zeros((BLK, ncols), jnp.float32)
        return 0

    pl.semaphore_wait(barrier, 7)

    hops, settled, jobs, sends = plan(half)
    stages = len(hops)

    def at_stage(i):
        if i < len(HOPS):
            take_hop(*hops[i])
        if i == 0:
            lax.fori_loop(UPTO[0], NTILES, pack, 0, unroll=2)
        if i == 2:
            for load in loads[2:]:
                load.wait()
            lax.fori_loop(0, bdepth // BLK, mask_b, 0)
            for n in (0, 1, 4):
                b_out[n].start()
        if i == 3:
            lax.fori_loop(0, 16, zero, 0)
        if i % 3 == 0 and i < 3 * half:
            table_step(i // 3 + 1)
        if i == 13:
            for n in (0, 1):
                b_in[n].wait_recv()
            for n in (2, 3, 5, 6):
                b_out[n].start()
        if i == 18:
            for n in (2, 3):
                b_in[n].wait_recv()
            b_out[7].start()
        for q in settled[i]:
            settle(q)
        if i == READY:
            for n in range(4, 8):
                b_in[n].wait_recv()
            table_hop(0, half).wait_recv()

            def row(j, over):
                one = table[j]
                places_v[pl.ds(j, 1), :] = one[0:1, :]
                return jnp.maximum(over, one)

            flags[0] = lax.fori_loop(0, nz, row, jnp.zeros((8, 2 * BLK), jnp.int32))
            down = pltpu.make_async_copy(places_v, places, in_sem.at[6])
            down.start()
            down.wait()
        n, late = divmod(i - READY - 2, 4)
        if late == 0 and 0 <= n < len(rounds):
            if n:
                flags[n] = f_take(n - 1)
            for m in range(len(rounds[n][1])):
                f_copy(n, m).start()

    def after_stage(i):
        for q in range(3):
            if i == sends[q]:
                if q:
                    c_copy(0, q - 1).wait_recv()
                    acc[q, (q - 1) * hg : q * hg, :] += far[q - 1]
                for way in range(2):
                    c_copy(q, way).start()

    for i in range(stages):
        at_stage(i)
        if jobs[i] >= 0:
            work(jobs[i] // half, jobs[i] % half)
        after_stage(i)
    for q in (1, 2):
        for way in range(2):
            c_copy(q, way).wait_recv()
    for r in range(nb):
        at = pl.ds(r * BLK, BLK)
        part, sub = r // (nb // 2), pl.ds(r % (nb // 2) * BLK, BLK)
        for p in range(ncols // (2 * BLK)):
            ls = slice(p * 2 * BLK, (p + 1) * 2 * BLK)
            row = y * nb + r
            total = acc[3, at, ls] + got[0, part, sub, ls] + got[1, part, sub, ls]
            out_ref[at, ls] = total * pair(c_mask[2 * p, row], c_mask[2 * p + 1, row])
    flag_ref[...] = f_take(len(rounds) - 1)

    for h in range(1, half + 1):
        table_hop(0, h).wait_send()
        if h < half:
            table_hop(1, h).wait_send()
        for q in range(4):
            for s in range(2):
                for way in range(2):
                    if way == s or h < half:
                        hop(way, q, s, h).wait_send()
    for copy in b_out:
        copy.wait_send()
    for q in range(3):
        for way in range(2):
            c_copy(q, way).wait_send()
    for n in range(len(rounds)):
        for m in range(len(rounds[n][1])):
            f_copy(n, m).wait_send()


def dense(nz, nx, ny, a_blocks, a_mask, b_blocks, b_mask, c_mask):
    rows, depth = a_blocks.shape
    bdepth, ncols = b_blocks.shape
    grp = rows // ny
    half = nz // 2
    vmem, smem = pl.BlockSpec(memory_space=pltpu.VMEM), pl.BlockSpec(memory_space=pltpu.SMEM)
    dma = pltpu.SemaphoreType.DMA
    return pl.pallas_call(
        functools.partial(dense_kernel, nz, nx, ny),
        out_shape=jax.ShapeDtypeStruct((grp, ncols), jnp.float32),
        in_specs=[smem, smem, smem, vmem, vmem],
        out_specs=vmem,
        scratch_shapes=[
            pltpu.VMEM((rows, depth), jnp.bfloat16),
            pltpu.VMEM((2, half, rows, depth), jnp.bfloat16),
            pltpu.VMEM((2 * nx * bdepth, ncols), jnp.bfloat16),
            pltpu.VMEM((ny, grp, ncols), jnp.float32),
            pltpu.VMEM((ny - 1, grp, ncols), jnp.float32),
            dma((2, ny, 2, half)),
            dma((2, ny, 2, half)),
            dma((8,)),
            dma((8,)),
            dma((ny - 1,)),
            dma((ny - 1,)),
        ],
        compiler_params=pltpu.CompilerParams(
            collective_id=1, has_side_effects=True, vmem_limit_bytes=40 * 2**20
        ),
    )(a_mask, b_mask, c_mask, a_blocks, b_blocks)


def compact(nz, nx, ny, a_blocks, a_mask, b_blocks, b_mask, c_mask):
    rows, depth = a_blocks.shape
    bdepth, ncols = b_blocks.shape
    grp = rows // ny
    half = nz // 2
    vmem, anywhere = pl.BlockSpec(memory_space=pltpu.VMEM), pl.BlockSpec(memory_space=pl.ANY)
    dma = pltpu.SemaphoreType.DMA
    return pl.pallas_call(
        functools.partial(compact_kernel, nz, nx, ny),
        out_shape=(
            jax.ShapeDtypeStruct((grp, ncols), jnp.float32),
            jax.ShapeDtypeStruct((8, 128), jnp.int32),
        ),
        in_specs=[anywhere] * 5,
        out_specs=(vmem, vmem),
        scratch_shapes=[
            pltpu.SMEM(a_mask.shape[::-1], jnp.int32),
            pltpu.SMEM(b_mask.shape, jnp.int32),
            pltpu.SMEM(c_mask.shape[::-1], jnp.int32),
            pltpu.VMEM((rows, depth), jnp.bfloat16),
            pltpu.VMEM((bdepth, ncols), jnp.bfloat16),
            pltpu.VMEM((rows * depth // (2 * BLK * BLK), BLK, 2 * BLK), jnp.bfloat16),
            pltpu.VMEM((8, 128), jnp.int32),
            pltpu.SMEM((8, 128), jnp.int32),
            pltpu.VMEM((nz, 128), jnp.int32),
            pltpu.SMEM((nz, 128), jnp.int32),
            pltpu.VMEM((nz, NTILES, BLK, 2 * BLK), jnp.bfloat16),
            pltpu.VMEM((nz, 8, 128), jnp.int32),
            pltpu.VMEM((2 * nx * bdepth, ncols), jnp.bfloat16),
            pltpu.VMEM((nz, NTILES, BLK, 2 * BLK), jnp.bfloat16),
            pltpu.VMEM((grp, 2 * depth), jnp.bfloat16),
            pltpu.VMEM((ny, grp, ncols), jnp.float32),
            pltpu.VMEM((2, grp // 2, ncols), jnp.float32),
            pltpu.VMEM((2, 2, grp // 2, ncols), jnp.float32),
            pltpu.VMEM((5, 8, 128), jnp.int32),
            pltpu.VMEM((5, 2, 8, 128), jnp.int32),
            dma((7,)),
            dma((2, half)),
            dma((2, half)),
            dma((2, 4, 2, half)),
            dma((2, 4, 2, half)),
            dma((8,)),
            dma((8,)),
            dma((2, 3)),
            dma((2, 3)),
            dma((5, 2)),
            dma((5, 2)),
        ],
        compiler_params=pltpu.CompilerParams(
            collective_id=0, has_side_effects=True, vmem_limit_bytes=40 * 2**20
        ),
    )(a_mask.T, b_mask, c_mask.T, a_blocks, b_blocks)


def shards(nz, nx, ny, *args):
    product, flag = compact(nz, nx, ny, *args)
    return lax.cond(flag[1, 0] > 0, lambda: dense(nz, nx, ny, *args), lambda: product)


def solution(mesh):
    nz, ncol, ny = mesh.shape["row"], mesh.shape["col"], mesh.shape["layer"]
    in_specs = (
        P("col", ("layer", "row")),
        P("col", ("layer", "row")),
        P(("layer", "col"), "row"),
        P(("layer", "col"), "row"),
        P("col", "row"),
    )
    out_specs = P(("col", "layer"), "row")
    body = functools.partial(shards, nz, ncol // 2, ny)
    return jax.shard_map(body, mesh=mesh, in_specs=in_specs, out_specs=out_specs, check_vma=False)
```

```python
import functools

import jax
import jax.numpy as jnp
from jax import lax
from jax.experimental import pallas as pl
from jax.experimental.pallas import tpu as pltpu
from jax.sharding import PartitionSpec as P

BLK = 64
MESH = pl.DeviceIdType.MESH
ORDER = (1, 3, 2, 0)

TILES = ((4, 4), (4, 4), (3, 2), (3, 2))
NTILES = sum(map(sum, TILES))
UPTO = tuple(sum(map(sum, TILES[: q + 1])) for q in range(4))

READY = 24

HOPS = (
    0, 3, 1, 0, 3, 1, 0, 2, 3, 1, 0, 2, 3, 1, 0, 2, 3, 1, 0, 4, 2, 3, 1, 0, 5, 4, 2, 3, 1, 0,
    5, 4, 6, 2, 5, 4, 7, 6, 2, 5, 4, 7, 6, 2, 5, 4, 7, 6, 5, 4, 7, 6, 5, 4, 7, 6, 7, 6, 7, 6,
)


def plan(half):
    taken, hops, settled, jobs, sends = [0] * 8, [], [], [], []
    done, worked = set(), set()
    last = [max(i for i, chunk in enumerate(HOPS) if chunk // 2 == q) for q in range(4)]
    todo = [(q, w % half) for q in range(4) for w in range(1, half + 1)]
    i = 0
    while len(worked) < len(todo):
        hops.append(None)
        if i < len(HOPS):
            chunk = HOPS[i]
            taken[chunk] += 1
            hops[i] = (chunk // 2, chunk % 2, taken[chunk])
        settled.append([q for q in range(4) if q not in done and i >= min(last[q] + 2, len(HOPS) + (q == 3))])
        done.update(settled[i])
        arrived = [half if q in done else min(taken[2 * q], taken[2 * q + 1]) - 1 for q in range(4)]
        job = -1
        for q, w in todo:
            if (
                i >= READY
                and (q, w) not in worked
                and (w or half) <= arrived[q]
                and (q == 0 or (q - 1, w) in worked)
            ):
                job = q * half + w
                worked.add((q, w))
                break
        jobs.append(job)
        for q in range(3):
            if len(sends) == q and all((q, w) in worked for w in range(half)):
                sends.append(max(i, sends[-1] + 3) if sends else i)
        i += 1
    return hops, settled, jobs, sends


def wrap(value, size):
    return lax.rem(value + size, size)


def dense_kernel(
    nz, nx, ny,
    a_mask, b_mask, c_mask, a_ref, b_ref, out_ref,
    am, g, bf, acc, got,
    a_send, a_recv, b_send, b_recv, c_send, c_recv,
):
    z, col, y = lax.axis_index("row"), lax.axis_index("col"), lax.axis_index("layer")
    x, core = col // 2, lax.rem(col, 2)
    half = nz // 2
    rows, depth = a_ref.shape
    grp = rows // ny
    sub = grp // 2
    bdepth, ncols = b_ref.shape

    zs = (wrap(z + 1, nz), wrap(z - 1, nz))
    xs = (wrap(x + 1, nx) * 2 + core, wrap(x - 1, nx) * 2 + core)
    sib = x * 2 + 1 - core
    opp = wrap(x + 2, nx) * 2 + core

    barrier = pltpu.get_barrier_semaphore()
    for peer in zs:
        pl.semaphore_signal(barrier, inc=1, device_id={"row": peer}, device_id_type=MESH)
    for peer in xs + (sib,):
        pl.semaphore_signal(barrier, inc=1, device_id={"col": peer}, device_id_type=MESH)
    for d in range(1, ny):
        pl.semaphore_signal(barrier, inc=1, device_id={"layer": wrap(y + d, ny)}, device_id_type=MESH)

    lane = lax.broadcasted_iota(jnp.int32, (1, 2 * BLK), 1)

    def pair(m0, m1):
        return jnp.where(lane < BLK, m0, m1).astype(jnp.float32)

    def group_of(q):
        d = jnp.where(q == 0, ORDER[0], jnp.where(q == 1, ORDER[1], jnp.where(q == 2, ORDER[2], 0)))
        return wrap(y + d, ny), d

    nb = grp // BLK
    def mask_a(t, _):
        q, r = t // nb, lax.rem(t, nb)
        src = group_of(q)[0] * nb + r
        at = pl.ds(pl.multiple_of(src * BLK, BLK), BLK)
        to = pl.ds(pl.multiple_of(t * BLK, BLK), BLK)
        for p in range(depth // (2 * BLK)):
            ls = slice(p * 2 * BLK, (p + 1) * 2 * BLK)
            m = pair(a_mask[src, 2 * p], a_mask[src, 2 * p + 1]).astype(am.dtype)
            am[to, ls] = a_ref[at, ls] * m
        return 0
    lax.fori_loop(0, rows // BLK, mask_a, 0)

    def mask_b(t, _):
        at = pl.ds(pl.multiple_of(t * BLK, BLK), BLK)
        to = pl.ds(pl.multiple_of(col * bdepth + t * BLK, BLK), BLK)
        for p in range(ncols // (2 * BLK)):
            ls = slice(p * 2 * BLK, (p + 1) * 2 * BLK)
            m = pair(b_mask[t, 2 * p], b_mask[t, 2 * p + 1]).astype(bf.dtype)
            bf[to, ls] = b_ref[at, ls] * m
        return 0
    lax.fori_loop(0, bdepth // BLK, mask_b, 0)

    pl.semaphore_wait(barrier, 5 + ny - 1)

    def chunk(ref, q, s):
        return ref.at[pl.ds(pl.multiple_of(q * grp + s * sub, sub), sub)]

    def hop(way, q, s, h):
        dst = chunk(g.at[way, h - 1], q, s)
        return dst, pltpu.make_async_remote_copy(
            src_ref=dst, dst_ref=dst,
            send_sem=a_send.at[way, q, s, h - 1], recv_sem=a_recv.at[way, q, s, h - 1],
            device_id={"row": zs[way]}, device_id_type=MESH,
        )

    def start_hop(way, q, s, h):
        dst = chunk(g.at[way, h - 1], q, s)
        def go(src):
            pltpu.make_async_remote_copy(
                src_ref=src, dst_ref=dst,
                send_sem=a_send.at[way, q, s, h - 1], recv_sem=a_recv.at[way, q, s, h - 1],
                device_id={"row": zs[way]}, device_id_type=MESH,
            ).start()
        @pl.when(h == 1)
        def _():
            go(chunk(am, q, s))
        @pl.when(h > 1)
        def _():
            go(chunk(g.at[way, jnp.maximum(h - 2, 0)], q, s))

    def b_rows(owner, first, count):
        return bf.at[pl.ds(pl.multiple_of(owner * bdepth + first, count), count)]

    hb = bdepth // 2
    def b_copy(n, owner, first, count, peer):
        ref = b_rows(owner, first, count)
        return pltpu.make_async_remote_copy(
            src_ref=ref, dst_ref=ref, send_sem=b_send.at[n], recv_sem=b_recv.at[n],
            device_id={"col": peer}, device_id_type=MESH,
        )

    b_out = (
        b_copy(0, col, 0, bdepth, xs[0]),
        b_copy(1, col, 0, bdepth, xs[1]),
        b_copy(2, xs[1], 0, hb, xs[0]),
        b_copy(3, xs[0], hb, hb, xs[1]),
        b_copy(4, col, 0, bdepth, sib),
        b_copy(5, xs[1], 0, bdepth, sib),
        b_copy(6, xs[0], 0, bdepth, sib),
        b_copy(7, opp, 0, bdepth, sib),
    )
    other = 1 - 2 * core
    b_in = (
        b_copy(0, xs[1], 0, bdepth, xs[0]),
        b_copy(1, xs[0], 0, bdepth, xs[1]),
        b_copy(2, opp, 0, hb, xs[0]),
        b_copy(3, opp, hb, hb, xs[1]),
        b_copy(4, sib, 0, bdepth, sib),
        b_copy(5, xs[1] + other, 0, bdepth, sib),
        b_copy(6, xs[0] + other, 0, bdepth, sib),
        b_copy(7, opp + other, 0, bdepth, sib),
    )

    def c_copy(q):
        target, d = group_of(q)
        return pltpu.make_async_remote_copy(
            src_ref=acc.at[q], dst_ref=got.at[q], send_sem=c_send.at[q], recv_sem=c_recv.at[q],
            device_id={"layer": target}, device_id_type=MESH,
        )

    def b_of(source):
        return bf[pl.ds(pl.multiple_of(source * depth, depth), depth), :]

    def dot(a, b):
        return jnp.dot(a, b, preferred_element_type=jnp.float32)

    def work(q, h):
        @pl.when(h == 0)
        def _():
            acc[q] = dot(am[pl.ds(pl.multiple_of(q * grp, grp), grp), :], b_of(z))
        @pl.when((h > 0) & (h < half))
        def _():
            at = pl.ds(pl.multiple_of(q * grp, grp), grp)
            n = jnp.maximum(h - 1, 0)
            acc[q] += dot(g[0, n, at, :], b_of(wrap(z - h, nz))) + dot(g[1, n, at, :], b_of(wrap(z + h, nz)))
        @pl.when(h == half)
        def _():
            source = b_of(wrap(z + half, nz))
            for s in range(2):
                at = pl.ds(pl.multiple_of(q * grp + s * sub, sub), sub)
                to = pl.ds(s * sub, sub)
                acc[q, to, :] += dot(g[s, half - 1, at, :], source)

    def settle(q):
        for s in range(2):
            hop(s, q, s, half)[1].wait_recv()

    def step(t, _):
        q, h = t // half, lax.rem(t, half) + 1
        for s in range(2):
            for way in range(2):
                @pl.when(h > 1)
                def _():
                    hop(way, q, s, jnp.maximum(h - 1, 1))[1].wait_recv()
                if way == s:
                    start_hop(way, q, s, h)
                else:
                    @pl.when(h < half)
                    def _():
                        start_hop(way, q, s, h)

        @pl.when(t == 0)
        def _():
            for n in (0, 1, 4):
                b_out[n].start()

        @pl.when((q == 0) & (h == 6))
        def _():
            for n in (0, 1):
                b_in[n].wait_recv()
            for n in (2, 3, 5, 6):
                b_out[n].start()

        @pl.when((q >= 1) & (h == 1))
        def _():
            settle(q - 1)

        @pl.when((q == 1) & (h == 1))
        def _():
            for n in (2, 3):
                b_in[n].wait_recv()
            b_out[7].start()
            for n in range(4, 8):
                b_in[n].wait_recv()

        @pl.when(q >= 1)
        def _():
            @pl.when((h == 1) & (q >= 2))
            def _():
                work(q - 1, half)
                c_copy(q - 1).start()
            work(q, h - 1)

        @pl.when(q == 1)
        def _():
            work(0, h - 1)
            @pl.when(h == half)
            def _():
                work(0, half)
                c_copy(0).start()
        return 0

    lax.fori_loop(0, ny * half, step, 0)
    last = ny - 1
    settle(last)
    work(last, half)
    for q in range(last):
        c_copy(q).wait_recv()
    for r in range(nb):
        at = pl.ds(r * BLK, BLK)
        for p in range(ncols // (2 * BLK)):
            ls = slice(p * 2 * BLK, (p + 1) * 2 * BLK)
            row = y * nb + r
            total = acc[last, at, ls] + got[0, at, ls] + got[1, at, ls] + got[2, at, ls]
            out_ref[at, ls] = total * pair(c_mask[row, 2 * p], c_mask[row, 2 * p + 1])

    def sent(t, _):
        q, h = t // half, lax.rem(t, half) + 1
        for s in range(2):
            for way in range(2):
                if way == s:
                    hop(way, q, s, h)[1].wait_send()
                else:
                    @pl.when(h < half)
                    def _():
                        hop(way, q, s, h)[1].wait_send()
        return 0
    lax.fori_loop(0, ny * half, sent, 0)
    for copy in b_out:
        copy.wait_send()
    for q in range(last):
        c_copy(q).wait_send()


def span(q, s):
    return sum(map(sum, TILES[:q])) + sum(TILES[q][:s]), TILES[q][s]


def compact_kernel(
    nz, nx, ny,
    a_mask_hbm, b_mask_hbm, c_mask_hbm, a_hbm, b_hbm, out_ref, flag_ref,
    a_mask, b_mask, c_mask, a_ref, b_ref, a_tiles, codes_v, codes, places_v, places,
    ring, table, bf, staged, wide, acc, far, got, flags, flag_in,
    in_sem, t_send, t_recv, a_send, a_recv, b_send, b_recv, c_send, c_recv, f_send, f_recv,
):
    z, col, y = lax.axis_index("row"), lax.axis_index("col"), lax.axis_index("layer")
    x, core = col // 2, lax.rem(col, 2)
    half = nz // 2
    rows, depth = a_ref.shape
    bdepth, ncols = b_ref.shape
    grp = rows // ny
    nb = grp // BLK
    nk = depth // BLK

    loads = [
        pltpu.make_async_copy(src, dst, in_sem.at[n])
        for n, (src, dst) in enumerate(
            ((a_mask_hbm, a_mask), (a_hbm, a_ref), (b_mask_hbm, b_mask), (b_hbm, b_ref), (c_mask_hbm, c_mask))
        )
    ]
    for load in loads:
        load.start()

    zs = (wrap(z + 1, nz), wrap(z - 1, nz))
    ys = (wrap(y + 1, ny), wrap(y - 1, ny))
    xs = (wrap(x + 1, nx) * 2 + core, wrap(x - 1, nx) * 2 + core)
    sib = x * 2 + 1 - core
    opp = wrap(x + 2, nx) * 2 + core

    barrier = pltpu.get_barrier_semaphore()
    for axis, peers in (("row", zs), ("col", xs + (sib,)), ("layer", ys)):
        for peer in peers:
            pl.semaphore_signal(barrier, inc=1, device_id={axis: peer}, device_id_type=MESH)

    lane = lax.broadcasted_iota(jnp.int32, (1, 2 * BLK), 1)

    def pair(m0, m1):
        return jnp.where(lane < BLK, m0, m1).astype(jnp.float32)

    def listed(n):
        q, i = n // nb, lax.rem(n, nb)
        low = i < nb // 2
        d = jnp.where(q == 0, 2, jnp.where(q == 3, 0, jnp.where(low, 1, 3)))
        r = jnp.where(q == 1, lax.rem(i, nb // 2), jnp.where(q == 2, nb // 2 + lax.rem(i, nb // 2), i))
        return wrap(y + d, ny) * nb + r

    loads[0].wait()

    def listing(t, carry):
        run, tile, side, bad, order, shift, place = carry
        n, k = t // nk, lax.rem(t, nk)
        row = listed(n)
        m = a_mask[k, row]
        order = jnp.where(lane == run, row * (nk // 2) + k // 2, order)
        shift = jnp.where(lane == run, lax.rem(k, 2), shift)
        place = jnp.where(lane == t, jnp.minimum(tile, NTILES - 1), place)
        place = jnp.where(lane == t + BLK, m * (1 + side), place)
        run, tile, side = run + m, tile + m * side, side + m - 2 * m * side
        q = n // nb
        most = jnp.where(q == 0, UPTO[0], jnp.where(q == 1, UPTO[1], jnp.where(q == 2, UPTO[2], UPTO[3]))) * 2
        bad = jnp.where(run > most, 1, bad)
        return run, tile, side, bad, order, shift, place

    nothing = jnp.zeros((1, 2 * BLK), jnp.int32)
    _, _, _, bad, order, shift, place = lax.fori_loop(
        0, rows // BLK * nk, listing, (0, 0, 0, 0, nothing, nothing, nothing), unroll=8
    )
    sub8 = lax.broadcasted_iota(jnp.int32, (8, 2 * BLK), 0)
    codes_v[...] = jnp.where(sub8 == 0, order, shift)
    table[0] = jnp.where(sub8 == 0, place, bad)
    to_smem = pltpu.make_async_copy(codes_v, codes, in_sem.at[5])
    to_smem.start()
    loads[1].wait()

    def tiled(row, _):
        for p in range(nk // 2):
            a_tiles[row * (nk // 2) + p] = a_ref[
                pl.ds(pl.multiple_of(row * BLK, BLK), BLK), p * 2 * BLK : (p + 1) * 2 * BLK
            ]
        return 0

    lax.fori_loop(0, rows // BLK, tiled, 0, unroll=4)
    to_smem.wait()

    lanes = lax.broadcasted_iota(jnp.int32, (BLK, 2 * BLK), 1)

    def side_by_side(left, right, stay):
        kept = jnp.where(lanes < BLK, left, right)
        moved = pltpu.roll(jnp.where(lanes < BLK, right, left), BLK, 1)
        return jnp.where(stay == 1, kept, moved)

    def pack(u, _):
        left, right = (a_tiles[codes[0, 2 * u + side]] for side in range(2))
        stay = jnp.where(lanes < BLK, 1 - codes[1, 2 * u], codes[1, 2 * u + 1])
        ring[0, u] = side_by_side(left, right, stay)
        return 0

    lax.fori_loop(0, UPTO[0], pack, 0, unroll=4)

    def slot(way, h):
        return h if h in (0, half) else half * way + h

    def hop(way, q, s, h):
        first, size = span(q, s)
        return pltpu.make_async_remote_copy(
            src_ref=ring.at[slot(way, h - 1), pl.ds(first, size)],
            dst_ref=ring.at[slot(way, h), pl.ds(first, size)],
            send_sem=a_send.at[way, q, s, h - 1], recv_sem=a_recv.at[way, q, s, h - 1],
            device_id={"row": zs[way]}, device_id_type=MESH,
        )

    def table_hop(way, h):
        return pltpu.make_async_remote_copy(
            src_ref=table.at[slot(way, h - 1)], dst_ref=table.at[slot(way, h)],
            send_sem=t_send.at[way, h - 1], recv_sem=t_recv.at[way, h - 1],
            device_id={"row": zs[way]}, device_id_type=MESH,
        )

    def b_rows(owner, first, count):
        return bf.at[pl.ds(pl.multiple_of(owner * bdepth + first, count), count)]

    hb = bdepth // 2

    def b_copy(n, owner, first, count, peer):
        ref = b_rows(owner, first, count)
        return pltpu.make_async_remote_copy(
            src_ref=ref, dst_ref=ref, send_sem=b_send.at[n], recv_sem=b_recv.at[n],
            device_id={"col": peer}, device_id_type=MESH,
        )

    b_out = (
        b_copy(0, col, 0, bdepth, xs[0]),
        b_copy(1, col, 0, bdepth, xs[1]),
        b_copy(2, xs[1], 0, hb, xs[0]),
        b_copy(3, xs[0], hb, hb, xs[1]),
        b_copy(4, col, 0, bdepth, sib),
        b_copy(5, xs[1], 0, bdepth, sib),
        b_copy(6, xs[0], 0, bdepth, sib),
        b_copy(7, opp, 0, bdepth, sib),
    )
    other = 1 - 2 * core
    b_in = (
        b_copy(0, xs[1], 0, bdepth, xs[0]),
        b_copy(1, xs[0], 0, bdepth, xs[1]),
        b_copy(2, opp, 0, hb, xs[0]),
        b_copy(3, opp, hb, hb, xs[1]),
        b_copy(4, sib, 0, bdepth, sib),
        b_copy(5, xs[1] + other, 0, bdepth, sib),
        b_copy(6, xs[0] + other, 0, bdepth, sib),
        b_copy(7, opp + other, 0, bdepth, sib),
    )

    def mask_b(t, _):
        at = pl.ds(pl.multiple_of(t * BLK, BLK), BLK)
        to = pl.ds(pl.multiple_of(col * bdepth + t * BLK, BLK), BLK)
        for p in range(ncols // (2 * BLK)):
            ls = slice(p * 2 * BLK, (p + 1) * 2 * BLK)
            m = pair(b_mask[t, 2 * p], b_mask[t, 2 * p + 1]).astype(bf.dtype)
            bf[to, ls] = b_ref[at, ls] * m
        return 0

    hg = grp // 2

    def c_copy(q, way):
        return pltpu.make_async_remote_copy(
            src_ref=acc.at[q, pl.ds(way * hg, hg)],
            dst_ref=far.at[way] if q == 0 else got.at[way, q - 1],
            send_sem=c_send.at[way, q], recv_sem=c_recv.at[way, q],
            device_id={"layer": ys[way]}, device_id_type=MESH,
        )

    rounds = (("col", xs), ("col", xs), ("col", (sib,)), ("layer", ys), ("layer", ys))

    def f_copy(n, m):
        axis, peers = rounds[n]
        return pltpu.make_async_remote_copy(
            src_ref=flags.at[n], dst_ref=flag_in.at[n, m], send_sem=f_send.at[n, m], recv_sem=f_recv.at[n, m],
            device_id={axis: peers[m]}, device_id_type=MESH,
        )

    def f_take(n):
        value = flags[n]
        for m in range(len(rounds[n][1])):
            f_copy(n, m).wait_recv()
            value = jnp.maximum(value, flag_in[n, m])
        return value

    def settle(q):
        for s in range(2):
            hop(s, q, s, half).wait_recv()
            hop(1 - s, q, s, half - 1).wait_recv()

    def table_step(h):
        for way in range(2):
            if h > 1:
                table_hop(way, h - 1).wait_recv()
            if way == 0 or h < half:
                table_hop(way, h).start()

    def take_hop(q, s, h):
        for way in range(2):
            piece = s if way == 0 else 1 - s
            if h > 1:
                hop(way, q, piece, h - 1).wait_recv()
            hop(way, q, piece, h).start()

    def b_of(source):
        return bf[pl.ds(pl.multiple_of(source * depth, depth), depth), :]

    def work(q, w):
        first, size = span(q, 0)[0], sum(TILES[q])
        for j in range(2):
            staged[w + half * j, first : first + size] = ring[w + half * j, first : first + size]
        for i in range(nb):
            for j in range(2):
                for p in range(nk // 2):
                    here, t = w + half * j, q * (nb * nk) + i * nk + 2 * p
                    left, right = (staged[here, places[here, t + side]] for side in range(2))
                    at_left, at_right = places[here, t + BLK], places[here, t + 1 + BLK]
                    kept = pair(jnp.where(at_left == 1, 1, 0), jnp.where(at_right == 2, 1, 0)).astype(wide.dtype)
                    moved = pair(jnp.where(at_left == 2, 1, 0), jnp.where(at_right == 1, 1, 0)).astype(wide.dtype)
                    to = (2 * j + p) * 2 * BLK
                    wide[i * BLK : (i + 1) * BLK, to : to + 2 * BLK] = (
                        jnp.where(lanes < BLK, left, right) * kept
                        + pltpu.roll(jnp.where(lanes < BLK, right, left), BLK, 1) * moved
                    )
        second = z + (w or half)
        acc[q] += jnp.dot(
            wide[:, :depth], b_of(wrap(z - w, nz)), preferred_element_type=jnp.float32
        ) + jnp.dot(wide[:, depth:], b_of(wrap(second, nz)), preferred_element_type=jnp.float32)

    def zero(t, _):
        acc[t // 4, pl.ds(pl.multiple_of(lax.rem(t, 4) * BLK, BLK), BLK), :] = jnp.zeros((BLK, ncols), jnp.float32)
        return 0

    pl.semaphore_wait(barrier, 7)

    hops, settled, jobs, sends = plan(half)
    stages = len(hops)

    def at_stage(i):
        if i < len(HOPS):
            take_hop(*hops[i])
        if i == 0:
            lax.fori_loop(UPTO[0], NTILES, pack, 0, unroll=2)
        if i == 1:
            for load in loads[2:]:
                load.wait()
            lax.fori_loop(0, bdepth // BLK, mask_b, 0)
            for n in (0, 1, 4):
                b_out[n].start()
        if i == 22:
            lax.fori_loop(0, 16, zero, 0)
        if i % 3 == 0 and i < 3 * half:
            table_step(i // 3 + 1)
        if i == 13:
            for n in (0, 1):
                b_in[n].wait_recv()
            for n in (2, 3, 5, 6):
                b_out[n].start()
        if i == 18:
            for n in (2, 3):
                b_in[n].wait_recv()
            b_out[7].start()
        for q in settled[i]:
            settle(q)
        if i == READY:
            for n in range(4, 8):
                b_in[n].wait_recv()
            table_hop(0, half).wait_recv()

            def row(j, over):
                one = table[j]
                places_v[pl.ds(j, 1), :] = one[0:1, :]
                return jnp.maximum(over, one)

            flags[0] = lax.fori_loop(0, nz, row, jnp.zeros((8, 2 * BLK), jnp.int32))
            down = pltpu.make_async_copy(places_v, places, in_sem.at[6])
            down.start()
            down.wait()
        n, late = divmod(i - READY - 2, 4)
        if late == 0 and 0 <= n < len(rounds):
            if n:
                flags[n] = f_take(n - 1)
            for m in range(len(rounds[n][1])):
                f_copy(n, m).start()

    def after_stage(i):
        for q in range(3):
            if i == sends[q]:
                if q:
                    c_copy(0, q - 1).wait_recv()
                    acc[q, (q - 1) * hg : q * hg, :] += far[q - 1]
                for way in range(2):
                    c_copy(q, way).start()

    for i in range(stages):
        at_stage(i)
        if jobs[i] >= 0:
            work(jobs[i] // half, jobs[i] % half)
        after_stage(i)
    for q in (1, 2):
        for way in range(2):
            c_copy(q, way).wait_recv()
    for r in range(nb):
        at = pl.ds(r * BLK, BLK)
        part, sub = r // (nb // 2), pl.ds(r % (nb // 2) * BLK, BLK)
        for p in range(ncols // (2 * BLK)):
            ls = slice(p * 2 * BLK, (p + 1) * 2 * BLK)
            row = y * nb + r
            total = acc[3, at, ls] + got[0, part, sub, ls] + got[1, part, sub, ls]
            out_ref[at, ls] = total * pair(c_mask[2 * p, row], c_mask[2 * p + 1, row])
    flag_ref[...] = f_take(len(rounds) - 1)

    for h in range(1, half + 1):
        table_hop(0, h).wait_send()
        if h < half:
            table_hop(1, h).wait_send()
        for q in range(4):
            for s in range(2):
                for way in range(2):
                    if way == s or h < half:
                        hop(way, q, s, h).wait_send()
    for copy in b_out:
        copy.wait_send()
    for q in range(3):
        for way in range(2):
            c_copy(q, way).wait_send()
    for n in range(len(rounds)):
        for m in range(len(rounds[n][1])):
            f_copy(n, m).wait_send()


def dense(nz, nx, ny, a_blocks, a_mask, b_blocks, b_mask, c_mask):
    rows, depth = a_blocks.shape
    bdepth, ncols = b_blocks.shape
    grp = rows // ny
    half = nz // 2
    vmem, smem = pl.BlockSpec(memory_space=pltpu.VMEM), pl.BlockSpec(memory_space=pltpu.SMEM)
    dma = pltpu.SemaphoreType.DMA
    return pl.pallas_call(
        functools.partial(dense_kernel, nz, nx, ny),
        out_shape=jax.ShapeDtypeStruct((grp, ncols), jnp.float32),
        in_specs=[smem, smem, smem, vmem, vmem],
        out_specs=vmem,
        scratch_shapes=[
            pltpu.VMEM((rows, depth), jnp.bfloat16),
            pltpu.VMEM((2, half, rows, depth), jnp.bfloat16),
            pltpu.VMEM((2 * nx * bdepth, ncols), jnp.bfloat16),
            pltpu.VMEM((ny, grp, ncols), jnp.float32),
            pltpu.VMEM((ny - 1, grp, ncols), jnp.float32),
            dma((2, ny, 2, half)),
            dma((2, ny, 2, half)),
            dma((8,)),
            dma((8,)),
            dma((ny - 1,)),
            dma((ny - 1,)),
        ],
        compiler_params=pltpu.CompilerParams(
            collective_id=1, has_side_effects=True, vmem_limit_bytes=40 * 2**20
        ),
    )(a_mask, b_mask, c_mask, a_blocks, b_blocks)


def compact(nz, nx, ny, a_blocks, a_mask, b_blocks, b_mask, c_mask):
    rows, depth = a_blocks.shape
    bdepth, ncols = b_blocks.shape
    grp = rows // ny
    half = nz // 2
    vmem, anywhere = pl.BlockSpec(memory_space=pltpu.VMEM), pl.BlockSpec(memory_space=pl.ANY)
    dma = pltpu.SemaphoreType.DMA
    return pl.pallas_call(
        functools.partial(compact_kernel, nz, nx, ny),
        out_shape=(
            jax.ShapeDtypeStruct((grp, ncols), jnp.float32),
            jax.ShapeDtypeStruct((8, 128), jnp.int32),
        ),
        in_specs=[anywhere] * 5,
        out_specs=(vmem, vmem),
        scratch_shapes=[
            pltpu.SMEM(a_mask.shape[::-1], jnp.int32),
            pltpu.SMEM(b_mask.shape, jnp.int32),
            pltpu.SMEM(c_mask.shape[::-1], jnp.int32),
            pltpu.VMEM((rows, depth), jnp.bfloat16),
            pltpu.VMEM((bdepth, ncols), jnp.bfloat16),
            pltpu.VMEM((rows * depth // (2 * BLK * BLK), BLK, 2 * BLK), jnp.bfloat16),
            pltpu.VMEM((8, 128), jnp.int32),
            pltpu.SMEM((8, 128), jnp.int32),
            pltpu.VMEM((nz, 128), jnp.int32),
            pltpu.SMEM((nz, 128), jnp.int32),
            pltpu.VMEM((nz, NTILES, BLK, 2 * BLK), jnp.bfloat16),
            pltpu.VMEM((nz, 8, 128), jnp.int32),
            pltpu.VMEM((2 * nx * bdepth, ncols), jnp.bfloat16),
            pltpu.VMEM((nz, NTILES, BLK, 2 * BLK), jnp.bfloat16),
            pltpu.VMEM((grp, 2 * depth), jnp.bfloat16),
            pltpu.VMEM((ny, grp, ncols), jnp.float32),
            pltpu.VMEM((2, grp // 2, ncols), jnp.float32),
            pltpu.VMEM((2, 2, grp // 2, ncols), jnp.float32),
            pltpu.VMEM((5, 8, 128), jnp.int32),
            pltpu.VMEM((5, 2, 8, 128), jnp.int32),
            dma((7,)),
            dma((2, half)),
            dma((2, half)),
            dma((2, 4, 2, half)),
            dma((2, 4, 2, half)),
            dma((8,)),
            dma((8,)),
            dma((2, 3)),
            dma((2, 3)),
            dma((5, 2)),
            dma((5, 2)),
        ],
        compiler_params=pltpu.CompilerParams(
            collective_id=0, has_side_effects=True, vmem_limit_bytes=40 * 2**20
        ),
    )(a_mask.T, b_mask, c_mask.T, a_blocks, b_blocks)


def shards(nz, nx, ny, *args):
    product, flag = compact(nz, nx, ny, *args)
    return lax.cond(flag[1, 0] > 0, lambda: dense(nz, nx, ny, *args), lambda: product)


def solution(mesh):
    nz, ncol, ny = mesh.shape["row"], mesh.shape["col"], mesh.shape["layer"]
    in_specs = (
        P("col", ("layer", "row")),
        P("col", ("layer", "row")),
        P(("layer", "col"), "row"),
        P(("layer", "col"), "row"),
        P("col", "row"),
    )
    out_specs = P(("col", "layer"), "row")
    body = functools.partial(shards, nz, ncol // 2, ny)
    return jax.shard_map(body, mesh=mesh, in_specs=in_specs, out_specs=out_specs, check_vma=False)
```
